512 devices in a mesh: guide: 2 (over core), seq: 32 (over z, x), rep: 8 (over y).
Axes of the slice: x: 4, y: 8, z: 8, core: 2. Of those that a mesh axis runs over, the one named last changes fastest.
Arguments:
- queries: bfloat16 [2, 32768, 1536], P('guide', ('rep', 'seq')), parts along dimension 1, may hold values from -125 to 125
- keys: bfloat16 [2, 32768, 1536], P('guide', ('rep', 'seq')), parts along dimension 1, may hold values from -4.5 to 4.5
- values: bfloat16 [2, 32768, 1536], P('guide', ('rep', 'seq')), parts along dimension 1, may hold values from -6 to 6
- hidden_in: bfloat16 [2, 32768, 3072], P(None, ('rep', 'seq'), 'guide'), parts along dimension 1, may hold values from -6 to 6
- out_weight: bfloat16 [1536, 3072], P(None, ('guide', 'seq')), may hold values from -0.15625 to 0.15625
- final_weight: bfloat16 [3072, 64], replicated, may hold values from -0.109375 to 0.109375
- gate_mod: bfloat16 [2, 40, 3072], P(None, 'rep'), parts along dimension 1, may hold values from -4 to 4
- span_tiles: int32 [40], P('rep'), parts along dimension 0, may hold values from 1 to 8, 32 in all
- text_len: int32 [2, 40], P(None, 'rep'), parts along dimension 1, may hold values from 1 to 128
- guide_on: int32 [40], P('rep'), parts along dimension 0, may hold values 0 or 1
- guide_scale: float32 [40], P('rep'), parts along dimension 0, may hold values from 2 to 7
- step_size: float32 [40], P('rep'), parts along dimension 0, may hold values from -0.6 to -0.1
- latent: float32 [32768, 64], P(('rep', 'seq')), parts along dimension 0, may hold values from -6 to 6
Outputs:
- latent_next: float32 [32768, 64], P(('rep', 'seq')), parts along dimension 0
The draws below stay inside these ranges and needn't reach their ends.
There are 8 independent parts, one for each index of `rep`. The reference program is written for one: setup_inputs(seed, part) draws one part's arguments, and reference() takes and returns one part's arrays. A program takes and returns all parts, laid end to end along the dimension named above; an argument that names none is the same for every part. Nothing has to cross between parts.
Inputs may be any that keep to these rules, and one draw needn't show every extreme that they name: `span_tiles`: some request spans exactly 8 tiles.
All inputs are finite; a program needn't handle non-finite values.
Results may differ from the reference program's by a relative error of at most 0.0011.
Values may be sent and summed in bfloat16 or wider, within the bound.
No kernel may reach another device: no remote copies, remote signals or barrier semaphores. Data moves between devices by JAX's collectives and lax.ppermute only.
A program may use at most 128 MiB of HBM per device.

```python
import math
import jax
import jax.numpy as jnp
import numpy as np
from jax import lax

D = 3072
HEAD_WIDTH = 128
OUT_CH = 64
TILE = 128
SPAN_MOST = 8
HD = 1536
TOKENS = 4096
TILES = 32
REQS = 5


def shared_keys(key):
    return jnp.clip(jax.random.normal(key, (2, TOKENS, HD), jnp.float32), -4.0, 4.0)


def draw_keys(key, part):
    base = shared_keys(key)
    return base.astype(jnp.bfloat16)


def draw_queries(key, part):
    key = jax.random.fold_in(key, 13)
    first = jax.random.fold_in(key, 0)
    result = jnp.clip(jax.random.normal(first, (2, TOKENS, HD), jnp.float32), -4.0, 4.0)
    return result.astype(jnp.bfloat16)


def touch_ends(drawn, key, least, top_value):
    shape = drawn.shape
    index_at = [jax.random.randint(jax.random.fold_in(key, axis), (), 0, shape[axis]) for axis in range(len(shape))]
    drawn = drawn.at[tuple(index_at)].set(least)
    longest = shape.index(max(shape))
    index_at[longest] = (index_at[longest] + 1) % shape[longest]
    return drawn.at[tuple(index_at)].set(top_value)


def steps_of(stream_key, extent, cuts, smallest, largest):
    level, own = 1.0, jax.random.fold_in(stream_key, 6)
    for axis_at, shards_of in cuts:
        draws = jnp.exp(jax.random.uniform(jax.random.fold_in(own, axis_at), (shards_of,), jnp.float32, smallest / len(cuts), largest / len(cuts)))
        level = level * jnp.repeat(draws, extent[axis_at] // shards_of).reshape([-1 if axis == axis_at else 1 for axis in range(len(extent))])
    return level


def profile(number_of, total, limit, lean):
    portions = [(1 << 20) // math.isqrt(standing ** lean) + 1 for standing in range(2, number_of + 1)]
    spare, holding = total - limit - (number_of - 1), [1] * (number_of - 1)
    while spare > 0:
        free = [i for i in range(number_of - 1) if holding[i] < limit]
        mass, budget = sum([portions[i] for i in free]), spare
        for i in free:
            extra = min(limit - holding[i], max(1, budget * portions[i] // mass), spare)
            holding[i] = holding[i] + extra
            spare = spare - extra
    return np.array([limit] + holding)


def uneven_parts(stream_key, count, total, most, slope):
    if count == 2:
        one = jax.random.randint(stream_key, (), max(1, total - most), min(most, total - 1) + 1)
        return jnp.stack([one, total - one])
    lengths = jnp.asarray(profile(count, total, most, slope), jnp.int32)
    twos = (count - 1) // 2
    donor, taker = lengths[1:1 + 2 * twos:2], lengths[2:2 + 2 * twos:2]
    margin = jnp.minimum(donor - 1, most - taker)
    shifted = jax.random.randint(jax.random.fold_in(stream_key, 1), (twos,), 0, 1 << 20) % (margin + 1)
    lengths = lengths.at[1:1 + 2 * twos:2].set(donor - shifted).at[2:2 + 2 * twos:2].set(taker + shifted)
    return lengths[jax.random.permutation(jax.random.fold_in(stream_key, 2), count)]


def scatter_about(own_key, shape, deviation, bound, pieces=(), kind=jnp.bfloat16):
    entries = deviation * jax.random.normal(own_key, shape, jnp.float32)
    if pieces:
        entries = entries * steps_of(own_key, shape, pieces, -0.22, 0.18)
    return jnp.clip(entries, -bound, bound).astype(kind)


def setup_inputs(seed: int = 0, part: int = 0) -> dict:
    arg_keys = jax.random.split(jax.random.key(seed), 14)
    part_keys = jax.random.split(jax.random.fold_in(arg_keys[13], part), 14)
    queries = draw_queries(jax.random.fold_in(jax.random.fold_in(arg_keys[13], part), 71), part)
    keys = draw_keys(jax.random.fold_in(jax.random.fold_in(arg_keys[13], part), 71), part)
    values = scatter_about(part_keys[2], (2, TOKENS, HD), 1.0, 6.0, ((0, 2), (1, 32)))
    hidden_in = scatter_about(part_keys[3], (2, TOKENS, D), 1.0, 6.0, ((1, 32), (2, 2)))
    out_weight = scatter_about(arg_keys[4], (HD, D), HD ** -0.5, 0.15625, ((1, 64),))
    final_weight = scatter_about(arg_keys[5], (D, OUT_CH), D ** -0.5, 0.109375)
    gate_mod = scatter_about(part_keys[6], (2, REQS, D), 1.0, 4.0)
    span_tiles = uneven_parts(part_keys[7], REQS, TILES, SPAN_MOST, 1).astype(jnp.int32)
    text_len = touch_ends(jax.random.randint(part_keys[8], (2, REQS), 1, TILE + 1), jax.random.fold_in(part_keys[8], 1), 1, TILE).astype(jnp.int32)
    guide_on = touch_ends((jax.random.randint(part_keys[9], (REQS,), 0, 4) < 3).astype(jnp.int32), jax.random.fold_in(part_keys[9], 1), 0, 1)
    guide_scale = jnp.clip(jnp.exp(jax.random.uniform(part_keys[10], (REQS,), jnp.float32, math.log(2.0), math.log(7.0))), 2.0, 7.0)
    step_size = jnp.clip(jax.random.uniform(part_keys[11], (REQS,), jnp.float32, -0.6, -0.1), -0.6, -0.1)
    latent = scatter_about(part_keys[12], (TOKENS, OUT_CH), 1.0, 6.0, ((0, 32),), jnp.float32)
    return dict(queries=queries, keys=keys, values=values, hidden_in=hidden_in, out_weight=out_weight, final_weight=final_weight, gate_mod=gate_mod, span_tiles=span_tiles, text_len=text_len, guide_on=guide_on, guide_scale=guide_scale, step_size=step_size, latent=latent)


def layout(positions, span_tiles, text_lens, total):
    ends = jnp.cumsum(span_tiles).astype(jnp.int32)
    starts = (ends - span_tiles).astype(jnp.int32)
    tile_of = positions // TILE
    inside = (positions >= 0) & (positions < total)
    member = (tile_of[:, None] >= starts[None, :]) & (tile_of[:, None] < ends[None, :]) & inside[:, None]
    first = lax.optimization_barrier(jnp.sum(jnp.where(member, starts[None, :], 0), axis=1)) * TILE
    tlen = lax.optimization_barrier(jnp.sum(jnp.where(member, text_lens[None, :], 0), axis=1))
    offset = positions - first
    live = jnp.any(member, axis=1) & ((offset >= TILE) | (offset < tlen))
    return (member, live)

def attend(query, key_rows, value_rows, member_q, member_k, live_k):
    count = query.shape[0]
    width = key_rows.shape[0]
    query_heads = query.reshape(count, -1, HEAD_WIDTH).astype(jnp.float32)
    key_heads = key_rows.reshape(width, -1, HEAD_WIDTH).astype(jnp.float32)
    value_heads = value_rows.reshape(width, -1, HEAD_WIDTH).astype(jnp.float32)
    same = jnp.dot(member_q.astype(jnp.float32), member_k.astype(jnp.float32).T, precision=lax.Precision.HIGHEST) > 0.5
    allowed = same & live_k[None, :]
    attention_score = jnp.einsum('gkv,tkv->kgt', query_heads, key_heads) * HEAD_WIDTH ** (-0.5)
    attention_score = jnp.where(allowed[None], attention_score, -jnp.inf)
    top = lax.optimization_barrier(jnp.max(attention_score, axis=-1, keepdims=True))
    weight = jnp.exp(attention_score - top)
    total = lax.optimization_barrier(jnp.sum(weight, axis=-1))
    weight_second = weight.astype(jnp.bfloat16).astype(jnp.float32)
    mixed_output = jnp.einsum('ijx,xic->jic', weight_second, value_heads)
    return (mixed_output / total.T[:, :, None]).reshape(count, -1).astype(jnp.bfloat16)

def layer_norm(state):
    centre = state - lax.optimization_barrier(jnp.mean(state, axis=-1, keepdims=True))
    spread = lax.optimization_barrier(jnp.mean(centre * centre, axis=-1, keepdims=True))
    return centre * lax.rsqrt(spread + 1e-06)

def guide_mix(cond, uncond, switch, factor):
    blend = jnp.where(switch > 0, uncond + factor * (cond - uncond), cond)
    upper = jnp.sqrt(lax.optimization_barrier(jnp.mean(cond * cond, axis=-1, keepdims=True)) + 1e-06)
    lower = jnp.sqrt(lax.optimization_barrier(jnp.mean(blend * blend, axis=-1, keepdims=True)) + 1e-06)
    return blend * (upper / lower)

def per_token(member, table):
    return lax.optimization_barrier(jnp.sum(jnp.where(member, table[None, :], jnp.zeros_like(table)[None, :]), axis=1))[:, None]

def reference(queries, keys, values, hidden_in, out_weight, final_weight, gate_mod, span_tiles, text_len, guide_on, guide_scale, step_size, latent):
    total = queries.shape[1]
    positions = jnp.arange(total, dtype=jnp.int32)
    speeds = []
    member = None
    for half in range(2):
        member, live = layout(positions, span_tiles, text_len[half], total)
        q_tiles = queries[half].reshape(total // TILE, TILE, -1)
        m_tiles = member.reshape(total // TILE, TILE, -1)

        def one_tile(pair):
            return attend(pair[0], keys[half], values[half], pair[1], member, live)
        attn = lax.map(one_tile, (q_tiles, m_tiles)).reshape(total, -1)
        mixed_output = jnp.dot(attn, out_weight, preferred_element_type=jnp.float32)
        gate_rows = jnp.dot(member.astype(jnp.float32), gate_mod[half].astype(jnp.float32), precision=lax.Precision.HIGHEST)
        state = hidden_in[half].astype(jnp.float32) + gate_rows * mixed_output
        normed = layer_norm(state).astype(jnp.bfloat16)
        speeds.append(jnp.dot(normed, final_weight, preferred_element_type=jnp.float32))
    switch = per_token(member, guide_on)
    factor = per_token(member, guide_scale)
    stride = per_token(member, step_size)
    return latent + stride * guide_mix(speeds[0], speeds[1], switch, factor)
```

```python
import jax
import jax.numpy as jnp
from jax import lax
from jax.experimental import pallas as pl
from jax.experimental.pallas import tpu as pltpu
from jax.sharding import PartitionSpec as P

HEAD_WIDTH = 128
TILE = 128
SPAN_MOST = 8
FULL_WIDTH = 3072
ROW = 4
LOG2E = 1.4426950408889634
NT = (((1,), (1,)), ((), ()))


def swapped(value):
    return lax.ppermute(value, "guide", [(0, 1), (1, 0)])


def along_z(value, by):
    count = lax.axis_size("seq")
    step = by * ROW
    pairs = [(i, i + step) for i in range(count) if 0 <= i + step < count]
    return lax.ppermute(value, "seq", pairs)


def spread(value):
    count = lax.axis_size("seq")
    groups = [[z * ROW + x for x in range(ROW)] for z in range(count // ROW)]
    return lax.all_to_all(value, "seq", 0, 0, axis_index_groups=groups)


def by_features(value):
    rows, width = value.shape
    return value.reshape(rows, ROW, width // ROW).transpose(1, 0, 2)


def request_of(tile, spans, tables):
    start = jnp.int32(0)
    found = [jnp.int32(0) for _ in range(len(tables) + 3)]
    for r in range(spans.shape[0]):
        span = spans[r]
        here = (tile >= start) & (tile < start + span)
        row = [start, span, jnp.int32(r)] + [table(r) for table in tables]
        found = [jnp.where(here, new, old) for new, old in zip(row, found)]
        start = start + span
    return found


def attend_kernel(
    where, spans, text_len, q_ref, far_l, near_l, own, near_r, far_r, o_ref, k_all, v_all
):
    place, half = where[0], where[1]
    first = (place // ROW) * ROW
    heads = q_ref.shape[2] // HEAD_WIDTH
    at = 0
    for ref in (far_l, near_l, own, near_r, far_r):
        for i in range(ref.shape[0]):
            k_all[at * TILE : (at + 1) * TILE, :] = ref[i, 0]
            v_all[at * TILE : (at + 1) * TILE, :] = ref[i, 1]
            at += 1
    keys = SPAN_MOST * TILE
    column = lax.broadcasted_iota(jnp.int32, (1, keys), 1)
    factor = HEAD_WIDTH**-0.5 * LOG2E
    for t in range(ROW):
        start, span, _, live = request_of(first + t, spans, [lambda r: text_len[half, r]])
        begin = jnp.clip(start - (first - (SPAN_MOST - 1)), 0, SPAN_MOST + ROW - 2)
        begin = pl.multiple_of(begin * TILE, TILE)
        allowed = ((column < live) | (column >= TILE)) & (column < span * TILE)
        bias = jnp.where(allowed, 0.0, -1e30)
        for h in range(heads):
            lanes = slice(h * HEAD_WIDTH, (h + 1) * HEAD_WIDTH)
            key = k_all[pl.ds(begin, keys), lanes]
            value = v_all[pl.ds(begin, keys), lanes]
            score = lax.dot_general(
                q_ref[t, :, lanes], key, NT, preferred_element_type=jnp.float32
            )
            score = score + bias
            top = jnp.max(score, axis=-1, keepdims=True)
            weight = jnp.exp2((score - top) * factor)
            total = jnp.sum(weight, axis=-1, keepdims=True)
            mixed = jnp.dot(weight.astype(jnp.bfloat16), value, preferred_element_type=jnp.float32)
            o_ref[t, :, lanes] = (mixed / total).astype(jnp.bfloat16)


def attend(where, spans, text_len, q, far_l, near_l, own, near_r, far_r):
    rows = (SPAN_MOST * 2 + ROW - 2) * TILE
    width = q.shape[2]
    smem = pl.BlockSpec(memory_space=pltpu.SMEM)
    vmem = pl.BlockSpec(memory_space=pltpu.VMEM)
    pairs = ROW * TILE * SPAN_MOST * TILE * (width // HEAD_WIDTH)
    return pl.pallas_call(
        attend_kernel,
        out_shape=jax.ShapeDtypeStruct(q.shape, jnp.bfloat16),
        in_specs=[smem] * 3 + [vmem] * 6,
        out_specs=vmem,
        scratch_shapes=[
            pltpu.VMEM((rows, width), jnp.bfloat16),
            pltpu.VMEM((rows, width), jnp.bfloat16),
        ],
        compiler_params=pltpu.CompilerParams(vmem_limit_bytes=40 << 20),
        cost_estimate=pl.CostEstimate(
            flops=4 * pairs * HEAD_WIDTH, bytes_accessed=8 << 20, transcendentals=pairs
        ),
        name="attend",
    )(where, spans, text_len, q, far_l, near_l, own, near_r, far_r)


def project_kernel(
    where, spans, mine, theirs, w_ref, hidden, gate, final_t, sums, colsum, state
):
    step = pl.program_id(0)
    place, half = where[0], where[1]
    _, _, request = request_of(place, spans, [])
    block = w_ref.shape[0]
    width = state.shape[2]
    here = pl.multiple_of(half * width + step * block, 128)
    groups, _, depth = mine.shape
    for side, source in enumerate((mine, theirs)):
        which = half if side == 0 else 1 - half
        total = jnp.zeros((TILE, block), jnp.float32)
        for j in range(groups):
            total += lax.dot_general(
                source[j],
                w_ref[:, j * depth : (j + 1) * depth],
                NT,
                preferred_element_type=jnp.float32,
            )
        scale = jnp.zeros((1, block), jnp.float32)
        for r in range(gate.shape[1]):
            row = gate[which, r : r + 1, pl.ds(here, block)].astype(jnp.float32)
            scale = jnp.where(request == r, row, scale)
        state[which, :, pl.ds(pl.multiple_of(step * block, 128), block)] = (
            hidden[which].astype(jnp.float32) + scale * total
        )

    @pl.when(step == 0)
    def _():
        ones = jnp.ones((8, width), jnp.bfloat16)
        other = pl.multiple_of((1 - half) * width, 128)
        base = pl.multiple_of(half * width, 128)
        mine_sum = lax.dot_general(
            ones, final_t[:, pl.ds(base, width)], NT, preferred_element_type=jnp.float32
        )
        other_sum = lax.dot_general(
            ones, final_t[:, pl.ds(other, width)], NT, preferred_element_type=jnp.float32
        )
        colsum[...] = mine_sum - other_sum

    @pl.when(step == pl.num_programs(0) - 1)
    def _():
        weights = final_t[:, pl.ds(pl.multiple_of(half * width, 128), width)]
        channels = weights.shape[0]
        lane = lax.broadcasted_iota(jnp.int32, (TILE, sums.shape[2] - channels), 1)
        for which in range(2):
            rows = state[which]
            mean = jnp.mean(rows, axis=-1, keepdims=True)
            centre = rows - mean
            squares = jnp.sum(centre * centre, axis=-1, keepdims=True)
            high = centre.astype(jnp.bfloat16)
            low = (centre - high.astype(jnp.float32)).astype(jnp.bfloat16)
            speed = lax.dot_general(high, weights, NT, preferred_element_type=jnp.float32)
            speed += lax.dot_general(low, weights, NT, preferred_element_type=jnp.float32)
            sums[which, :, :channels] = speed
            sums[which, :, channels:] = jnp.where(
                lane == 0, mean, jnp.where(lane == 1, squares, 0.0)
            )


def project(where, spans, mine, theirs, weight_t, hidden, gate, final_t):
    steps = 4
    depth, width = weight_t.shape[1], weight_t.shape[0]
    block = width // steps
    channels = final_t.shape[0]
    smem = pl.BlockSpec(memory_space=pltpu.SMEM)
    vmem = pl.BlockSpec(memory_space=pltpu.VMEM)
    return pl.pallas_call(
        project_kernel,
        grid=(steps,),
        out_shape=(
            jax.ShapeDtypeStruct((2, TILE, 2 * channels), jnp.float32),
            jax.ShapeDtypeStruct((8, channels), jnp.float32),
        ),
        in_specs=[
            smem,
            smem,
            vmem,
            vmem,
            pl.BlockSpec((block, depth), lambda i: (i, 0)),
            pl.BlockSpec((2, TILE, block), lambda i: (0, 0, i)),
            vmem,
            vmem,
        ],
        out_specs=(vmem, vmem),
        scratch_shapes=[pltpu.VMEM((2, TILE, width), jnp.float32)],
        compiler_params=pltpu.CompilerParams(vmem_limit_bytes=40 << 20),
        cost_estimate=pl.CostEstimate(
            flops=4 * TILE * depth * width, bytes_accessed=8 << 20, transcendentals=0
        ),
        name="project",
    )(where, spans, mine, theirs, weight_t, hidden, gate, final_t)


def finish_kernel(where, spans, on, scales, strides, mine, theirs, colsum, latent_t, out_t):
    _, _, _, switch, factor, stride = request_of(
        where[0], spans, [lambda r: on[r], lambda r: scales[r], lambda r: strides[r]]
    )
    channels = latent_t.shape[0]
    full = FULL_WIDTH
    speeds = []
    for which in range(2):
        a, b = mine[which], theirs[which]
        gap = a[:, channels : channels + 1] - b[:, channels : channels + 1]
        squares = a[:, channels + 1 : channels + 2] + b[:, channels + 1 : channels + 2]
        spread_of = squares + gap * gap * (full / 4)
        raw = a[:, :channels] + b[:, :channels] + (0.5 * gap) * colsum[0:1, :]
        speeds.append(raw * lax.rsqrt(spread_of / full + 1e-06))
    cond, uncond = speeds
    blend = jnp.where(switch > 0, uncond + factor * (cond - uncond), cond)
    upper = jnp.sqrt(jnp.mean(cond * cond, axis=-1, keepdims=True) + 1e-06)
    lower = jnp.sqrt(jnp.mean(blend * blend, axis=-1, keepdims=True) + 1e-06)
    out_t[...] = latent_t[...] + (stride * (blend * (upper / lower))).T


def finish(where, spans, on, scales, strides, mine, theirs, colsum, latent_t):
    smem = pl.BlockSpec(memory_space=pltpu.SMEM)
    vmem = pl.BlockSpec(memory_space=pltpu.VMEM)
    return pl.pallas_call(
        finish_kernel,
        out_shape=jax.ShapeDtypeStruct(latent_t.shape, jnp.float32),
        in_specs=[smem] * 5 + [vmem] * 4,
        out_specs=vmem,
        name="finish",
    )(where, spans, on, scales, strides, mine, theirs, colsum, latent_t)


def shards(
    queries,
    keys,
    values,
    hidden_in,
    out_weight,
    final_weight,
    gate_mod,
    span_tiles,
    text_len,
    guide_on,
    guide_scale,
    step_size,
    latent,
):
    place = lax.axis_index("seq")
    half = lax.axis_index("guide")
    where = jnp.stack([place, half]).astype(jnp.int32)
    weight_t = lax.all_gather(out_weight.T, "seq", axis=0, tiled=True)

    own = spread(jnp.stack([by_features(keys[0]), by_features(values[0])], axis=1))
    near_l = along_z(own, 1)
    near_r = along_z(own, -1)
    q_sent, _ = lax.optimization_barrier((by_features(queries[0]), own))
    q = spread(q_sent)
    far_l = along_z(near_l[1:], 1)
    far_r = along_z(near_r[:-1], -1)
    attn = spread(attend(where, span_tiles, text_len, q, far_l, near_l, own, near_r, far_r))
    theirs = swapped(attn)
    sums, colsum = project(
        where, span_tiles, attn, theirs, weight_t, hidden_in, gate_mod, final_weight.T
    )
    out_t = finish(
        where, span_tiles, guide_on, guide_scale, step_size, sums, swapped(sums), colsum, latent.T
    )
    return out_t.T


def solution(mesh):
    in_specs = (
        P("guide", ("rep", "seq"), None),
        P("guide", ("rep", "seq"), None),
        P("guide", ("rep", "seq"), None),
        P(None, ("rep", "seq"), "guide"),
        P(None, ("guide", "seq")),
        P(),
        P(None, "rep", None),
        P("rep"),
        P(None, "rep"),
        P("rep"),
        P("rep"),
        P("rep"),
        P(("rep", "seq"), None),
    )
    out_specs = P(("rep", "seq"), None)
    return jax.shard_map(shards, mesh=mesh, in_specs=in_specs, out_specs=out_specs, check_vma=False)
```

```python
import jax
import jax.numpy as jnp
from jax import lax
from jax.experimental import pallas as pl
from jax.experimental.pallas import tpu as pltpu
from jax.sharding import PartitionSpec as P

HEAD_WIDTH = 128
TILE = 128
SPAN_MOST = 8
FULL_WIDTH = 3072
ROW = 4
STEPS = 6
LOG2E = 1.4426950408889634
NT = (((1,), (1,)), ((), ()))


def swapped(value):
    return lax.ppermute(value, "guide", [(0, 1), (1, 0)])


def along_z(value, by):
    count = lax.axis_size("seq")
    step = by * ROW
    pairs = [(i, i + step) for i in range(count) if 0 <= i + step < count]
    return lax.ppermute(value, "seq", pairs)


def spread(value):
    count = lax.axis_size("seq")
    groups = [[z * ROW + x for x in range(ROW)] for z in range(count // ROW)]
    return lax.all_to_all(value, "seq", 0, 0, axis_index_groups=groups)


def pack_kernel(k_ref, v_ref, q_ref, kv_out, q_out):
    width = q_out.shape[2]
    for j in range(ROW):
        lanes = slice(j * width, (j + 1) * width)
        kv_out[j, 0] = k_ref[0, :, lanes]
        kv_out[j, 1] = v_ref[0, :, lanes]
        q_out[j] = q_ref[0, :, lanes]


def pack(keys, values, queries):
    _, rows, width = keys.shape
    vmem = pl.BlockSpec(memory_space=pltpu.VMEM)
    return pl.pallas_call(
        pack_kernel,
        out_shape=(
            jax.ShapeDtypeStruct((ROW, 2, rows, width // ROW), keys.dtype),
            jax.ShapeDtypeStruct((ROW, rows, width // ROW), queries.dtype),
        ),
        in_specs=[vmem] * 3,
        out_specs=(vmem, vmem),
        compiler_params=pltpu.CompilerParams(vmem_limit_bytes=8 << 20),
        name="pack",
    )(keys, values, queries)


def request_of(tile, spans, tables):
    start = jnp.int32(0)
    found = [jnp.int32(0) for _ in range(len(tables) + 3)]
    for r in range(spans.shape[0]):
        span = spans[r]
        here = (tile >= start) & (tile < start + span)
        row = [start, span, jnp.int32(r)] + [table(r) for table in tables]
        found = [jnp.where(here, new, old) for new, old in zip(row, found)]
        start = start + span
    return found


def attend_kernel(
    where, spans, text_len, q_ref, far_l, near_l, own, near_r, far_r, o_ref, k_all, v_all
):
    place, half = where[0], where[1]
    first = (place // ROW) * ROW
    heads = q_ref.shape[2] // HEAD_WIDTH
    at = 0
    for ref in (far_l, near_l, own, near_r, far_r):
        for i in range(ref.shape[0]):
            k_all[at * TILE : (at + 1) * TILE, :] = ref[i, 0]
            v_all[at * TILE : (at + 1) * TILE, :] = ref[i, 1]
            at += 1
    keys = SPAN_MOST * TILE
    column = lax.broadcasted_iota(jnp.int32, (1, keys), 1)
    factor = HEAD_WIDTH**-0.5 * LOG2E
    for t in range(ROW):
        start, span, _, live = request_of(first + t, spans, [lambda r: text_len[half, r]])
        begin = jnp.clip(start - (first - (SPAN_MOST - 1)), 0, SPAN_MOST + ROW - 2)
        begin = pl.multiple_of(begin * TILE, TILE)
        allowed = ((column < live) | (column >= TILE)) & (column < span * TILE)
        bias = jnp.where(allowed, 0.0, -1e30)
        for h in range(heads):
            lanes = slice(h * HEAD_WIDTH, (h + 1) * HEAD_WIDTH)
            key = k_all[pl.ds(begin, keys), lanes]
            value = v_all[pl.ds(begin, keys), lanes]
            score = lax.dot_general(
                q_ref[t, :, lanes], key, NT, preferred_element_type=jnp.float32
            )
            score = score + bias
            top = jnp.max(score, axis=-1, keepdims=True)
            weight = jnp.exp2((score - top) * factor)
            total = jnp.sum(weight, axis=-1, keepdims=True)
            mixed = jnp.dot(weight.astype(jnp.bfloat16), value, preferred_element_type=jnp.float32)
            o_ref[t, :, lanes] = (mixed / total).astype(jnp.bfloat16)


def attend(where, spans, text_len, q, far_l, near_l, own, near_r, far_r):
    rows = (SPAN_MOST * 2 + ROW - 2) * TILE
    width = q.shape[2]
    smem = pl.BlockSpec(memory_space=pltpu.SMEM)
    vmem = pl.BlockSpec(memory_space=pltpu.VMEM)
    pairs = ROW * TILE * SPAN_MOST * TILE * (width // HEAD_WIDTH)
    return pl.pallas_call(
        attend_kernel,
        out_shape=jax.ShapeDtypeStruct(q.shape, jnp.bfloat16),
        in_specs=[smem] * 3 + [vmem] * 6,
        out_specs=vmem,
        scratch_shapes=[
            pltpu.VMEM((rows, width), jnp.bfloat16),
            pltpu.VMEM((rows, width), jnp.bfloat16),
        ],
        compiler_params=pltpu.CompilerParams(vmem_limit_bytes=40 << 20),
        cost_estimate=pl.CostEstimate(
            flops=4 * pairs * HEAD_WIDTH, bytes_accessed=8 << 20, transcendentals=pairs
        ),
        name="attend",
    )(where, spans, text_len, q, far_l, near_l, own, near_r, far_r)


def project_kernel(
    where, spans, mine, theirs, w_ref, hidden, gate, final_t, sums, colsum, weight, state, arrived
):
    place, half = where[0], where[1]
    width = weight.shape[0]
    block = width // STEPS
    copies = [
        pltpu.make_async_copy(
            w_ref.at[pl.ds(c * block, block)], weight.at[pl.ds(c * block, block)], arrived.at[c]
        )
        for c in range(STEPS)
    ]
    for copy in copies:
        copy.start()

    _, _, request = request_of(place, spans, [])
    base = pl.multiple_of(half * width, 128)
    groups = mine.shape[0]
    attn = jnp.concatenate(
        [jnp.concatenate([source[j] for j in range(groups)], axis=1) for source in (mine, theirs)],
        axis=0,
    )
    weights = final_t[:, pl.ds(base, width)]
    others = final_t[:, pl.ds(pl.multiple_of((1 - half) * width, 128), width)]
    ones = jnp.ones((8, width), jnp.bfloat16)
    colsum[...] = lax.dot_general(
        ones, weights, NT, preferred_element_type=jnp.float32
    ) - lax.dot_general(ones, others, NT, preferred_element_type=jnp.float32)
    scales = []
    for which in (half, 1 - half):
        scale = jnp.zeros((1, width), jnp.float32)
        for r in range(gate.shape[1]):
            row = gate[which, r : r + 1, pl.ds(base, width)].astype(jnp.float32)
            scale = jnp.where(request == r, row, scale)
        scales.append(scale)

    for c in range(STEPS):
        copies[c].wait()
        here = slice(c * block, (c + 1) * block)
        total = lax.dot_general(attn, weight[here, :], NT, preferred_element_type=jnp.float32)
        for side, which in enumerate((half, 1 - half)):
            state[side, :, here] = (
                hidden[which, :, here].astype(jnp.float32)
                + scales[side][:, here] * total[side * TILE : (side + 1) * TILE]
            )

    channels = weights.shape[0]
    lane = lax.broadcasted_iota(jnp.int32, (TILE, sums.shape[2] - channels), 1)
    for side, which in enumerate((half, 1 - half)):
        rows = state[side]
        mean = jnp.mean(rows, axis=-1, keepdims=True)
        centre = rows - mean
        squares = jnp.sum(centre * centre, axis=-1, keepdims=True)
        high = centre.astype(jnp.bfloat16)
        low = (centre - high.astype(jnp.float32)).astype(jnp.bfloat16)
        speed = lax.dot_general(high, weights, NT, preferred_element_type=jnp.float32)
        speed += lax.dot_general(low, weights, NT, preferred_element_type=jnp.float32)
        sums[which, :, :channels] = speed
        sums[which, :, channels:] = jnp.where(
            lane == 0, mean, jnp.where(lane == 1, squares, 0.0)
        )


def project(where, spans, mine, theirs, weight_t, hidden, gate, final_t):
    depth, width = weight_t.shape[1], weight_t.shape[0]
    channels = final_t.shape[0]
    smem = pl.BlockSpec(memory_space=pltpu.SMEM)
    vmem = pl.BlockSpec(memory_space=pltpu.VMEM)
    return pl.pallas_call(
        project_kernel,
        out_shape=(
            jax.ShapeDtypeStruct((2, TILE, 2 * channels), jnp.float32),
            jax.ShapeDtypeStruct((8, channels), jnp.float32),
        ),
        in_specs=[smem, smem, vmem, vmem, pl.BlockSpec(memory_space=pl.ANY), vmem, vmem, vmem],
        out_specs=(vmem, vmem),
        scratch_shapes=[
            pltpu.VMEM((width, depth), jnp.bfloat16),
            pltpu.VMEM((2, TILE, width), jnp.float32),
            pltpu.SemaphoreType.DMA((STEPS,)),
        ],
        compiler_params=pltpu.CompilerParams(vmem_limit_bytes=56 << 20),
        cost_estimate=pl.CostEstimate(
            flops=4 * TILE * depth * width, bytes_accessed=8 << 20, transcendentals=0
        ),
        name="project",
    )(where, spans, mine, theirs, weight_t, hidden, gate, final_t)


def finish_kernel(where, spans, on, scales, strides, mine, theirs, colsum, latent_t, out_t):
    _, _, _, switch, factor, stride = request_of(
        where[0], spans, [lambda r: on[r], lambda r: scales[r], lambda r: strides[r]]
    )
    channels = latent_t.shape[0]
    full = FULL_WIDTH
    speeds = []
    for which in range(2):
        a, b = mine[which], theirs[which]
        gap = a[:, channels : channels + 1] - b[:, channels : channels + 1]
        squares = a[:, channels + 1 : channels + 2] + b[:, channels + 1 : channels + 2]
        spread_of = squares + gap * gap * (full / 4)
        raw = a[:, :channels] + b[:, :channels] + (0.5 * gap) * colsum[0:1, :]
        speeds.append(raw * lax.rsqrt(spread_of / full + 1e-06))
    cond, uncond = speeds
    blend = jnp.where(switch > 0, uncond + factor * (cond - uncond), cond)
    upper = jnp.sqrt(jnp.mean(cond * cond, axis=-1, keepdims=True) + 1e-06)
    lower = jnp.sqrt(jnp.mean(blend * blend, axis=-1, keepdims=True) + 1e-06)
    out_t[...] = latent_t[...] + (stride * (blend * (upper / lower))).T


def finish(where, spans, on, scales, strides, mine, theirs, colsum, latent_t):
    smem = pl.BlockSpec(memory_space=pltpu.SMEM)
    vmem = pl.BlockSpec(memory_space=pltpu.VMEM)
    return pl.pallas_call(
        finish_kernel,
        out_shape=jax.ShapeDtypeStruct(latent_t.shape, jnp.float32),
        in_specs=[smem] * 5 + [vmem] * 4,
        out_specs=vmem,
        compiler_params=pltpu.CompilerParams(vmem_limit_bytes=4 << 20),
        name="finish",
    )(where, spans, on, scales, strides, mine, theirs, colsum, latent_t)


def shards(
    queries,
    keys,
    values,
    hidden_in,
    out_weight,
    final_weight,
    gate_mod,
    span_tiles,
    text_len,
    guide_on,
    guide_scale,
    step_size,
    latent,
):
    place = lax.axis_index("seq")
    half = lax.axis_index("guide")
    where = jnp.stack([place, half]).astype(jnp.int32)
    weight_t = lax.all_gather(out_weight.T, "seq", axis=0, tiled=True)

    kv_sent, q_sent = pack(keys, values, queries)
    own = spread(kv_sent)
    near_l = along_z(own, 1)
    near_r = along_z(own, -1)
    q_sent, _ = lax.optimization_barrier((q_sent, own))
    q = spread(q_sent)
    far_l = along_z(near_l[1:], 1)
    far_r = along_z(near_r[:-1], -1)
    attn = spread(attend(where, span_tiles, text_len, q, far_l, near_l, own, near_r, far_r))
    theirs = swapped(attn)
    sums, colsum = project(
        where, span_tiles, attn, theirs, weight_t, hidden_in, gate_mod, final_weight.T
    )
    out_t = finish(
        where, span_tiles, guide_on, guide_scale, step_size, sums, swapped(sums), colsum, latent.T
    )
    return out_t.T


def solution(mesh):
    in_specs = (
        P("guide", ("rep", "seq"), None),
        P("guide", ("rep", "seq"), None),
        P("guide", ("rep", "seq"), None),
        P(None, ("rep", "seq"), "guide"),
        P(None, ("guide", "seq")),
        P(),
        P(None, "rep", None),
        P("rep"),
        P(None, "rep"),
        P("rep"),
        P("rep"),
        P("rep"),
        P(("rep", "seq"), None),
    )
    out_specs = P(("rep", "seq"), None)
    return jax.shard_map(shards, mesh=mesh, in_specs=in_specs, out_specs=out_specs, check_vma=False)
```

```python
import jax
import jax.numpy as jnp
from jax import lax
from jax.experimental import pallas as pl
from jax.experimental.pallas import tpu as pltpu
from jax.sharding import PartitionSpec as P

HEAD_WIDTH = 128
TILE = 128
SPAN_MOST = 8
FULL_WIDTH = 3072
ROW = 4
STEPS = 3
LOG2E = 1.4426950408889634
NT = (((1,), (1,)), ((), ()))


def swapped(value):
    return lax.ppermute(value, "guide", [(0, 1), (1, 0)])


def along_z(value, by):
    count = lax.axis_size("seq")
    step = by * ROW
    pairs = [(i, i + step) for i in range(count) if 0 <= i + step < count]
    return lax.ppermute(value, "seq", pairs)


def spread(value):
    count = lax.axis_size("seq")
    groups = [[z * ROW + x for x in range(ROW)] for z in range(count // ROW)]
    return lax.all_to_all(value, "seq", 0, 0, axis_index_groups=groups)


def pack_kernel(k_ref, v_ref, q_ref, kv_out, q_out):
    width = q_out.shape[2]
    for j in range(ROW):
        lanes = slice(j * width, (j + 1) * width)
        kv_out[j, 0] = k_ref[0, :, lanes]
        kv_out[j, 1] = v_ref[0, :, lanes]
        q_out[j] = q_ref[0, :, lanes]


def pack(keys, values, queries):
    _, rows, width = keys.shape
    vmem = pl.BlockSpec(memory_space=pltpu.VMEM)
    return pl.pallas_call(
        pack_kernel,
        out_shape=(
            jax.ShapeDtypeStruct((ROW, 2, rows, width // ROW), keys.dtype),
            jax.ShapeDtypeStruct((ROW, rows, width // ROW), queries.dtype),
        ),
        in_specs=[vmem] * 3,
        out_specs=(vmem, vmem),
        compiler_params=pltpu.CompilerParams(vmem_limit_bytes=8 << 20),
        name="pack",
    )(keys, values, queries)


def request_of(tile, spans, tables):
    start = jnp.int32(0)
    found = [jnp.int32(0) for _ in range(len(tables) + 3)]
    for r in range(spans.shape[0]):
        span = spans[r]
        here = (tile >= start) & (tile < start + span)
        row = [start, span, jnp.int32(r)] + [table(r) for table in tables]
        found = [jnp.where(here, new, old) for new, old in zip(row, found)]
        start = start + span
    return found


def attend_kernel(
    where, spans, text_len, q_ref, far_l, near_l, own, near_r, far_r, o_ref, k_all, v_all
):
    place, half = where[0], where[1]
    first = (place // ROW) * ROW
    heads = q_ref.shape[2] // HEAD_WIDTH
    at = 0
    for ref in (far_l, near_l, own, near_r, far_r):
        for i in range(ref.shape[0]):
            k_all[at * TILE : (at + 1) * TILE, :] = ref[i, 0]
            v_all[at * TILE : (at + 1) * TILE, :] = ref[i, 1]
            at += 1
    keys = SPAN_MOST * TILE
    column = lax.broadcasted_iota(jnp.int32, (1, keys), 1)
    factor = HEAD_WIDTH**-0.5 * LOG2E
    for t in range(ROW):
        start, span, _, live = request_of(first + t, spans, [lambda r: text_len[half, r]])
        begin = jnp.clip(start - (first - (SPAN_MOST - 1)), 0, SPAN_MOST + ROW - 2)
        begin = pl.multiple_of(begin * TILE, TILE)
        allowed = ((column < live) | (column >= TILE)) & (column < span * TILE)
        bias = jnp.where(allowed, 0.0, -1e30)
        for h in range(heads):
            lanes = slice(h * HEAD_WIDTH, (h + 1) * HEAD_WIDTH)
            key = k_all[pl.ds(begin, keys), lanes]
            value = v_all[pl.ds(begin, keys), lanes]
            score = lax.dot_general(
                q_ref[t, :, lanes], key, NT, preferred_element_type=jnp.float32
            )
            score = score + bias
            top = jnp.max(score, axis=-1, keepdims=True)
            weight = jnp.exp2((score - top) * factor)
            total = jnp.sum(weight, axis=-1, keepdims=True)
            mixed = jnp.dot(weight.astype(jnp.bfloat16), value, preferred_element_type=jnp.float32)
            o_ref[t, :, lanes] = (mixed / total).astype(jnp.bfloat16)


def attend(where, spans, text_len, q, far_l, near_l, own, near_r, far_r):
    rows = (SPAN_MOST * 2 + ROW - 2) * TILE
    width = q.shape[2]
    smem = pl.BlockSpec(memory_space=pltpu.SMEM)
    vmem = pl.BlockSpec(memory_space=pltpu.VMEM)
    pairs = ROW * TILE * SPAN_MOST * TILE * (width // HEAD_WIDTH)
    return pl.pallas_call(
        attend_kernel,
        out_shape=jax.ShapeDtypeStruct(q.shape, jnp.bfloat16),
        in_specs=[smem] * 3 + [vmem] * 6,
        out_specs=vmem,
        scratch_shapes=[
            pltpu.VMEM((rows, width), jnp.bfloat16),
            pltpu.VMEM((rows, width), jnp.bfloat16),
        ],
        compiler_params=pltpu.CompilerParams(vmem_limit_bytes=40 << 20),
        cost_estimate=pl.CostEstimate(
            flops=4 * pairs * HEAD_WIDTH, bytes_accessed=8 << 20, transcendentals=pairs
        ),
        name="attend",
    )(where, spans, text_len, q, far_l, near_l, own, near_r, far_r)


def prepare_kernel(
    where, spans, on, scales, strides, hidden, gate, final_t, latent_t, h_out, g_out, f_out, aux
):
    place, half = where[0], where[1]
    _, _, request, switch, factor, stride = request_of(
        place, spans, [lambda r: on[r], lambda r: scales[r], lambda r: strides[r]]
    )
    channels, width = f_out.shape
    base = pl.multiple_of(half * width, 128)
    for side, which in enumerate((half, 1 - half)):
        lanes = slice(side * TILE, (side + 1) * TILE)
        row = jnp.zeros((1, width), jnp.float32)
        for r in range(gate.shape[1]):
            new = gate[which, r : r + 1, pl.ds(base, width)].astype(jnp.float32)
            row = jnp.where(request == r, new, row)
        g_out[:, lanes] = jnp.broadcast_to(row, (TILE, width)).T.astype(jnp.bfloat16)
        h_out[:, lanes] = hidden[which].astype(jnp.float32).T.astype(jnp.bfloat16)
    weights = final_t[:, pl.ds(base, width)]
    others = final_t[:, pl.ds(pl.multiple_of((1 - half) * width, 128), width)]
    f_out[...] = weights
    ones = jnp.ones((width, TILE), jnp.bfloat16)
    aux[:channels] = latent_t[...]
    aux[channels : 2 * channels] = jnp.dot(
        weights, ones, preferred_element_type=jnp.float32
    ) - jnp.dot(others, ones, preferred_element_type=jnp.float32)
    line = lax.broadcasted_iota(jnp.int32, (8, TILE), 0)
    scalars = jnp.where(line == 1, factor, jnp.where(line == 2, stride, 0.0))
    aux[2 * channels :] = jnp.where(line == 0, switch.astype(jnp.float32), scalars)


def prepare(where, spans, on, scales, strides, hidden, gate, final_t, latent_t):
    width, channels = hidden.shape[2], final_t.shape[0]
    smem = pl.BlockSpec(memory_space=pltpu.SMEM)
    vmem = pl.BlockSpec(memory_space=pltpu.VMEM)
    turned = jax.ShapeDtypeStruct((width, 2 * TILE), jnp.bfloat16)
    return pl.pallas_call(
        prepare_kernel,
        out_shape=(
            turned,
            turned,
            jax.ShapeDtypeStruct((channels, width), jnp.bfloat16),
            jax.ShapeDtypeStruct((2 * channels + 8, TILE), jnp.float32),
        ),
        in_specs=[smem] * 5 + [vmem] * 4,
        out_specs=(vmem,) * 4,
        compiler_params=pltpu.CompilerParams(vmem_limit_bytes=20 << 20),
        name="prepare",
    )(where, spans, on, scales, strides, hidden, gate, final_t, latent_t)


def project_kernel(
    where, mine, theirs, w_ref, hidden, gate, final, sums, weight, attn, state, arrived
):
    half = where[1]
    width = weight.shape[0]
    block = width // STEPS
    copies = [
        pltpu.make_async_copy(
            w_ref.at[pl.ds(c * block, block)], weight.at[pl.ds(c * block, block)], arrived.at[c]
        )
        for c in range(STEPS)
    ]
    for copy in copies:
        copy.start()
    groups, _, depth = mine.shape
    for side, source in enumerate((mine, theirs)):
        for j in range(groups):
            attn[j * depth : (j + 1) * depth, side * TILE : (side + 1) * TILE] = source[j].T

    added = jnp.zeros((1, 2 * TILE), jnp.float32)
    for c in range(STEPS):
        copies[c].wait()
        here = slice(c * block, (c + 1) * block)
        total = jnp.dot(weight[here, :], attn[...], preferred_element_type=jnp.float32)
        new = hidden[here, :].astype(jnp.float32) + gate[here, :].astype(jnp.float32) * total
        state[here, :] = new
        added += jnp.sum(new, axis=0, keepdims=True)
    mean = added / width
    channels = final.shape[0]
    squares = jnp.zeros((1, 2 * TILE), jnp.float32)
    speed = jnp.zeros((channels, 2 * TILE), jnp.float32)
    for c in range(STEPS):
        here = slice(c * block, (c + 1) * block)
        centre = state[here, :] - mean
        squares += jnp.sum(centre * centre, axis=0, keepdims=True)
        high = centre.astype(jnp.bfloat16)
        low = (centre - high.astype(jnp.float32)).astype(jnp.bfloat16)
        speed += jnp.dot(final[:, here], high, preferred_element_type=jnp.float32)
        speed += jnp.dot(final[:, here], low, preferred_element_type=jnp.float32)
    line = lax.broadcasted_iota(jnp.int32, (8, 2 * TILE), 0)
    extra = jnp.where(line == 0, mean, jnp.where(line == 1, squares, 0.0))
    for side, which in enumerate((half, 1 - half)):
        lanes = slice(side * TILE, (side + 1) * TILE)
        sums[which, :channels] = speed[:, lanes]
        sums[which, channels:] = extra[:, lanes]


def project(where, mine, theirs, weight_t, hidden, gate, final):
    width, depth = weight_t.shape
    smem = pl.BlockSpec(memory_space=pltpu.SMEM)
    vmem = pl.BlockSpec(memory_space=pltpu.VMEM)
    return pl.pallas_call(
        project_kernel,
        out_shape=jax.ShapeDtypeStruct((2, final.shape[0] + 8, TILE), jnp.float32),
        in_specs=[smem, vmem, vmem, pl.BlockSpec(memory_space=pl.ANY), vmem, vmem, vmem],
        out_specs=vmem,
        scratch_shapes=[
            pltpu.VMEM((width, depth), jnp.bfloat16),
            pltpu.VMEM((depth, 2 * TILE), jnp.bfloat16),
            pltpu.VMEM((width, 2 * TILE), jnp.float32),
            pltpu.SemaphoreType.DMA((STEPS,)),
        ],
        compiler_params=pltpu.CompilerParams(vmem_limit_bytes=52 << 20),
        cost_estimate=pl.CostEstimate(
            flops=4 * TILE * depth * width, bytes_accessed=8 << 20, transcendentals=0
        ),
        name="project",
    )(where, mine, theirs, weight_t, hidden, gate, final)


def finish_kernel(a_ref, b_ref, aux, out_t):
    channels = out_t.shape[0]
    switch, factor, stride = (aux[2 * channels + i : 2 * channels + i + 1, :] for i in range(3))
    speeds = []
    for which in range(2):
        a, b = a_ref[which], b_ref[which]
        gap = a[channels : channels + 1] - b[channels : channels + 1]
        squares = a[channels + 1 : channels + 2] + b[channels + 1 : channels + 2]
        squares = squares + gap * gap * (FULL_WIDTH / 4)
        raw = a[:channels] + b[:channels] + (0.5 * gap) * aux[channels : 2 * channels, :]
        speeds.append(raw * lax.rsqrt(squares / FULL_WIDTH + 1e-06))
    cond, uncond = speeds
    blend = jnp.where(switch > 0, uncond + factor * (cond - uncond), cond)
    upper = jnp.sqrt(jnp.mean(cond * cond, axis=0, keepdims=True) + 1e-06)
    lower = jnp.sqrt(jnp.mean(blend * blend, axis=0, keepdims=True) + 1e-06)
    out_t[...] = aux[:channels, :] + stride * (blend * (upper / lower))


def finish(mine, theirs, aux, channels):
    vmem = pl.BlockSpec(memory_space=pltpu.VMEM)
    return pl.pallas_call(
        finish_kernel,
        out_shape=jax.ShapeDtypeStruct((channels, TILE), jnp.float32),
        in_specs=[vmem] * 3,
        out_specs=vmem,
        compiler_params=pltpu.CompilerParams(vmem_limit_bytes=4 << 20),
        name="finish",
    )(mine, theirs, aux)


def shards(
    queries,
    keys,
    values,
    hidden_in,
    out_weight,
    final_weight,
    gate_mod,
    span_tiles,
    text_len,
    guide_on,
    guide_scale,
    step_size,
    latent,
):
    place = lax.axis_index("seq")
    half = lax.axis_index("guide")
    where = jnp.stack([place, half]).astype(jnp.int32)
    weight_t = lax.all_gather(out_weight.T, "seq", axis=0, tiled=True)

    kv_sent, q_sent = pack(keys, values, queries)
    own = spread(kv_sent)
    near_l = along_z(own, 1)
    near_r = along_z(own, -1)
    q_sent, hidden_in, _ = lax.optimization_barrier((q_sent, hidden_in, own))
    q = spread(q_sent)
    far_l = along_z(near_l[1:], 1)
    far_r = along_z(near_r[:-1], -1)
    turned = prepare(
        where,
        span_tiles,
        guide_on,
        guide_scale,
        step_size,
        hidden_in,
        gate_mod,
        final_weight.T,
        latent.T,
    )
    q, (hidden, gate, final, aux) = lax.optimization_barrier((q, turned))
    attn = spread(attend(where, span_tiles, text_len, q, far_l, near_l, own, near_r, far_r))
    sums = project(where, attn, swapped(attn), weight_t, hidden, gate, final)
    return finish(sums, swapped(sums), aux, latent.shape[1]).T


def solution(mesh):
    in_specs = (
        P("guide", ("rep", "seq"), None),
        P("guide", ("rep", "seq"), None),
        P("guide", ("rep", "seq"), None),
        P(None, ("rep", "seq"), "guide"),
        P(None, ("guide", "seq")),
        P(),
        P(None, "rep", None),
        P("rep"),
        P(None, "rep"),
        P("rep"),
        P("rep"),
        P("rep"),
        P(("rep", "seq"), None),
    )
    out_specs = P(("rep", "seq"), None)
    return jax.shard_map(shards, mesh=mesh, in_specs=in_specs, out_specs=out_specs, check_vma=False)
```

```python
import jax
import jax.numpy as jnp
from jax import lax
from jax.experimental import pallas as pl
from jax.experimental.pallas import tpu as pltpu
from jax.sharding import PartitionSpec as P

HEAD_WIDTH = 128
TILE = 128
SPAN_MOST = 8
FULL_WIDTH = 3072
ROW = 4
STEPS = 4
LOG2E = 1.4426950408889634
NT = (((1,), (1,)), ((), ()))


def swapped(value):
    return lax.ppermute(value, "guide", [(0, 1), (1, 0)])


def along_z(value, by):
    count = lax.axis_size("seq")
    step = by * ROW
    pairs = [(i, i + step) for i in range(count) if 0 <= i + step < count]
    return lax.ppermute(value, "seq", pairs)


def spread(value):
    count = lax.axis_size("seq")
    groups = [[z * ROW + x for x in range(ROW)] for z in range(count // ROW)]
    return lax.all_to_all(value, "seq", 0, 0, axis_index_groups=groups)


def pack_kernel(k_ref, v_ref, q_ref, kv_out, q_out, sems):
    width = q_out.shape[2]
    copies = []
    for j in range(ROW):
        lanes = pl.ds(j * width, width)
        for source, target in (
            (k_ref, kv_out.at[j, 0]), (v_ref, kv_out.at[j, 1]), (q_ref, q_out.at[j])
        ):
            copies.append(
                pltpu.make_async_copy(source.at[0, :, lanes], target, sems.at[len(copies)])
            )
    for copy in copies:
        copy.start()
    for copy in copies:
        copy.wait()


def pack(keys, values, queries):
    _, rows, width = keys.shape
    vmem = pl.BlockSpec(memory_space=pltpu.VMEM)
    return pl.pallas_call(
        pack_kernel,
        out_shape=(
            jax.ShapeDtypeStruct((ROW, 2, rows, width // ROW), keys.dtype),
            jax.ShapeDtypeStruct((ROW, rows, width // ROW), queries.dtype),
        ),
        in_specs=[pl.BlockSpec(memory_space=pl.ANY)] * 3,
        out_specs=(vmem, vmem),
        scratch_shapes=[pltpu.SemaphoreType.DMA((3 * ROW,))],
        compiler_params=pltpu.CompilerParams(vmem_limit_bytes=56 << 20),
        name="pack",
    )(keys, values, queries)


def request_of(tile, spans, tables):
    start = jnp.int32(0)
    found = [jnp.int32(0) for _ in range(len(tables) + 3)]
    for r in range(spans.shape[0]):
        span = spans[r]
        here = (tile >= start) & (tile < start + span)
        row = [start, span, jnp.int32(r)] + [table(r) for table in tables]
        found = [jnp.where(here, new, old) for new, old in zip(row, found)]
        start = start + span
    return found


def attend_kernel(
    where, spans, text_len, q_ref, far_l, near_l, own, near_r, far_r, o_ref, k_all, v_all
):
    place, half = where[0], where[1]
    first = (place // ROW) * ROW
    heads = q_ref.shape[2] // HEAD_WIDTH
    at = 0
    for ref in (far_l, near_l, own, near_r, far_r):
        for i in range(ref.shape[0]):
            k_all[at * TILE : (at + 1) * TILE, :] = ref[i, 0]
            v_all[at * TILE : (at + 1) * TILE, :] = ref[i, 1]
            at += 1
    keys = SPAN_MOST * TILE
    column = lax.broadcasted_iota(jnp.int32, (1, keys), 1)
    factor = HEAD_WIDTH**-0.5 * LOG2E
    for t in range(ROW):
        start, span, _, live = request_of(first + t, spans, [lambda r: text_len[half, r]])
        begin = jnp.clip(start - (first - (SPAN_MOST - 1)), 0, SPAN_MOST + ROW - 2)
        begin = pl.multiple_of(begin * TILE, TILE)
        allowed = ((column < live) | (column >= TILE)) & (column < span * TILE)
        bias = jnp.where(allowed, 0.0, -1e30)
        for h in range(heads):
            lanes = slice(h * HEAD_WIDTH, (h + 1) * HEAD_WIDTH)
            key = k_all[pl.ds(begin, keys), lanes]
            value = v_all[pl.ds(begin, keys), lanes]
            score = lax.dot_general(
                q_ref[t, :, lanes], key, NT, preferred_element_type=jnp.float32
            )
            score = score + bias
            top = jnp.max(score, axis=-1, keepdims=True)
            weight = jnp.exp2((score - top) * factor)
            total = jnp.sum(weight, axis=-1, keepdims=True)
            mixed = jnp.dot(weight.astype(jnp.bfloat16), value, preferred_element_type=jnp.float32)
            o_ref[t, :, lanes] = (mixed / total).astype(jnp.bfloat16)


def attend(where, spans, text_len, q, far_l, near_l, own, near_r, far_r):
    rows = (SPAN_MOST * 2 + ROW - 2) * TILE
    width = q.shape[2]
    smem = pl.BlockSpec(memory_space=pltpu.SMEM)
    vmem = pl.BlockSpec(memory_space=pltpu.VMEM)
    pairs = ROW * TILE * SPAN_MOST * TILE * (width // HEAD_WIDTH)
    return pl.pallas_call(
        attend_kernel,
        out_shape=jax.ShapeDtypeStruct(q.shape, jnp.bfloat16),
        in_specs=[smem] * 3 + [vmem] * 6,
        out_specs=vmem,
        scratch_shapes=[
            pltpu.VMEM((rows, width), jnp.bfloat16),
            pltpu.VMEM((rows, width), jnp.bfloat16),
        ],
        compiler_params=pltpu.CompilerParams(vmem_limit_bytes=16 << 20),
        cost_estimate=pl.CostEstimate(
            flops=4 * pairs * HEAD_WIDTH, bytes_accessed=8 << 20, transcendentals=pairs
        ),
        name="attend",
    )(where, spans, text_len, q, far_l, near_l, own, near_r, far_r)


def prepare_kernel(
    where, spans, on, scales, strides, hidden, gate, final_t, latent_t, h_out, g_out, f_out, aux
):
    place, half = where[0], where[1]
    _, _, request, switch, factor, stride = request_of(
        place, spans, [lambda r: on[r], lambda r: scales[r], lambda r: strides[r]]
    )
    channels, width = f_out.shape
    base = pl.multiple_of(half * width, 128)
    for side, which in enumerate((half, 1 - half)):
        lanes = slice(side * TILE, (side + 1) * TILE)
        row = jnp.zeros((1, width), jnp.float32)
        for r in range(gate.shape[1]):
            new = gate[which, r : r + 1, pl.ds(base, width)].astype(jnp.float32)
            row = jnp.where(request == r, new, row)
        g_out[:, lanes] = jnp.broadcast_to(row, (TILE, width)).T.astype(jnp.bfloat16)
        h_out[:, lanes] = hidden[which].astype(jnp.float32).T.astype(jnp.bfloat16)
    weights = final_t[:, pl.ds(base, width)]
    others = final_t[:, pl.ds(pl.multiple_of((1 - half) * width, 128), width)]
    f_out[...] = weights
    ones = jnp.ones((width, TILE), jnp.bfloat16)
    aux[:channels] = latent_t[...]
    aux[channels : 2 * channels] = jnp.dot(
        weights, ones, preferred_element_type=jnp.float32
    ) - jnp.dot(others, ones, preferred_element_type=jnp.float32)
    line = lax.broadcasted_iota(jnp.int32, (8, TILE), 0)
    scalars = jnp.where(line == 1, factor, jnp.where(line == 2, stride, 0.0))
    aux[2 * channels :] = jnp.where(line == 0, switch.astype(jnp.float32), scalars)


def prepare(where, spans, on, scales, strides, hidden, gate, final_t, latent_t):
    width, channels = hidden.shape[2], final_t.shape[0]
    smem = pl.BlockSpec(memory_space=pltpu.SMEM)
    vmem = pl.BlockSpec(memory_space=pltpu.VMEM)
    turned = jax.ShapeDtypeStruct((width, 2 * TILE), jnp.bfloat16)
    return pl.pallas_call(
        prepare_kernel,
        out_shape=(
            turned,
            turned,
            jax.ShapeDtypeStruct((channels, width), jnp.bfloat16),
            jax.ShapeDtypeStruct((2 * channels + 8, TILE), jnp.float32),
        ),
        in_specs=[smem] * 5 + [vmem] * 4,
        out_specs=(vmem,) * 4,
        compiler_params=pltpu.CompilerParams(vmem_limit_bytes=16 << 20),
        name="prepare",
    )(where, spans, on, scales, strides, hidden, gate, final_t, latent_t)


def project_kernel(
    where, mine, theirs, w_ref, hidden, gate, final, sums, weight, attn, state, arrived
):
    half = where[1]
    width = weight.shape[0]
    block = width // STEPS
    copies = [
        pltpu.make_async_copy(
            w_ref.at[pl.ds(c * block, block)], weight.at[pl.ds(c * block, block)], arrived.at[c]
        )
        for c in range(STEPS)
    ]
    for copy in copies:
        copy.start()
    groups, _, depth = mine.shape
    for side, source in enumerate((mine, theirs)):
        for j in range(groups):
            attn[j * depth : (j + 1) * depth, side * TILE : (side + 1) * TILE] = source[j].T

    added = jnp.zeros((1, 2 * TILE), jnp.float32)
    for c in range(STEPS):
        copies[c].wait()
        here = slice(c * block, (c + 1) * block)
        total = jnp.dot(weight[here, :], attn[...], preferred_element_type=jnp.float32)
        new = hidden[here, :].astype(jnp.float32) + gate[here, :].astype(jnp.float32) * total
        state[here, :] = new
        added += jnp.sum(new, axis=0, keepdims=True)
    mean = added / width
    channels = final.shape[0]
    squares = jnp.zeros((1, 2 * TILE), jnp.float32)
    speed = jnp.zeros((channels, 2 * TILE), jnp.float32)
    for c in range(STEPS):
        here = slice(c * block, (c + 1) * block)
        centre = state[here, :] - mean
        squares += jnp.sum(centre * centre, axis=0, keepdims=True)
        high = centre.astype(jnp.bfloat16)
        low = (centre - high.astype(jnp.float32)).astype(jnp.bfloat16)
        speed += jnp.dot(final[:, here], high, preferred_element_type=jnp.float32)
        speed += jnp.dot(final[:, here], low, preferred_element_type=jnp.float32)
    line = lax.broadcasted_iota(jnp.int32, (8, 2 * TILE), 0)
    extra = jnp.where(line == 0, mean, jnp.where(line == 1, squares, 0.0))
    for side, which in enumerate((half, 1 - half)):
        lanes = slice(side * TILE, (side + 1) * TILE)
        sums[which, :channels] = speed[:, lanes]
        sums[which, channels:] = extra[:, lanes]


def project(where, mine, theirs, weight_t, hidden, gate, final):
    width, depth = weight_t.shape
    smem = pl.BlockSpec(memory_space=pltpu.SMEM)
    vmem = pl.BlockSpec(memory_space=pltpu.VMEM)
    return pl.pallas_call(
        project_kernel,
        out_shape=jax.ShapeDtypeStruct((2, final.shape[0] + 8, TILE), jnp.float32),
        in_specs=[smem, vmem, vmem, pl.BlockSpec(memory_space=pl.ANY), vmem, vmem, vmem],
        out_specs=vmem,
        scratch_shapes=[
            pltpu.VMEM((width, depth), jnp.bfloat16),
            pltpu.VMEM((depth, 2 * TILE), jnp.bfloat16),
            pltpu.VMEM((width, 2 * TILE), jnp.float32),
            pltpu.SemaphoreType.DMA((STEPS,)),
        ],
        compiler_params=pltpu.CompilerParams(vmem_limit_bytes=52 << 20),
        cost_estimate=pl.CostEstimate(
            flops=4 * TILE * depth * width, bytes_accessed=8 << 20, transcendentals=0
        ),
        name="project",
    )(where, mine, theirs, weight_t, hidden, gate, final)


def finish_kernel(a_ref, b_ref, aux, out_t):
    channels = out_t.shape[0]
    switch, factor, stride = (aux[2 * channels + i : 2 * channels + i + 1, :] for i in range(3))
    speeds = []
    for which in range(2):
        a, b = a_ref[which], b_ref[which]
        gap = a[channels : channels + 1] - b[channels : channels + 1]
        squares = a[channels + 1 : channels + 2] + b[channels + 1 : channels + 2]
        squares = squares + gap * gap * (FULL_WIDTH / 4)
        raw = a[:channels] + b[:channels] + (0.5 * gap) * aux[channels : 2 * channels, :]
        speeds.append(raw * lax.rsqrt(squares / FULL_WIDTH + 1e-06))
    cond, uncond = speeds
    blend = jnp.where(switch > 0, uncond + factor * (cond - uncond), cond)
    upper = jnp.sqrt(jnp.mean(cond * cond, axis=0, keepdims=True) + 1e-06)
    lower = jnp.sqrt(jnp.mean(blend * blend, axis=0, keepdims=True) + 1e-06)
    out_t[...] = aux[:channels, :] + stride * (blend * (upper / lower))


def finish(mine, theirs, aux, channels):
    vmem = pl.BlockSpec(memory_space=pltpu.VMEM)
    return pl.pallas_call(
        finish_kernel,
        out_shape=jax.ShapeDtypeStruct((channels, TILE), jnp.float32),
        in_specs=[vmem] * 3,
        out_specs=vmem,
        compiler_params=pltpu.CompilerParams(vmem_limit_bytes=4 << 20),
        name="finish",
    )(mine, theirs, aux)


def shards(
    queries,
    keys,
    values,
    hidden_in,
    out_weight,
    final_weight,
    gate_mod,
    span_tiles,
    text_len,
    guide_on,
    guide_scale,
    step_size,
    latent,
):
    place = lax.axis_index("seq")
    half = lax.axis_index("guide")
    where = jnp.stack([place, half]).astype(jnp.int32)
    weight_t = lax.all_gather(out_weight.T, "seq", axis=0, tiled=True)

    kv_sent, q_sent = pack(keys, values, queries)
    own = spread(kv_sent)
    near_l = along_z(own, 1)
    near_r = along_z(own, -1)
    q_sent, hidden_in, _ = lax.optimization_barrier((q_sent, hidden_in, own))
    q = spread(q_sent)
    far_l = along_z(near_l[1:], 1)
    far_r = along_z(near_r[:-1], -1)
    turned = prepare(
        where,
        span_tiles,
        guide_on,
        guide_scale,
        step_size,
        hidden_in,
        gate_mod,
        final_weight.T,
        latent.T,
    )
    q, (hidden, gate, final, aux) = lax.optimization_barrier((q, turned))
    attn = spread(attend(where, span_tiles, text_len, q, far_l, near_l, own, near_r, far_r))
    sums = project(where, attn, swapped(attn), weight_t, hidden, gate, final)
    return finish(sums, swapped(sums), aux, latent.shape[1]).T


def solution(mesh):
    in_specs = (
        P("guide", ("rep", "seq"), None),
        P("guide", ("rep", "seq"), None),
        P("guide", ("rep", "seq"), None),
        P(None, ("rep", "seq"), "guide"),
        P(None, ("guide", "seq")),
        P(),
        P(None, "rep", None),
        P("rep"),
        P(None, "rep"),
        P("rep"),
        P("rep"),
        P("rep"),
        P(("rep", "seq"), None),
    )
    out_specs = P(("rep", "seq"), None)
    return jax.shard_map(shards, mesh=mesh, in_specs=in_specs, out_specs=out_specs, check_vma=False)
```

```python
import jax
import jax.numpy as jnp
from jax import lax
from jax.experimental import pallas as pl
from jax.experimental.pallas import tpu as pltpu
from jax.sharding import PartitionSpec as P

HEAD_WIDTH = 128
TILE = 128
SPAN_MOST = 8
FULL_WIDTH = 3072
SHARD = 48
ROW = 4
LOG2E = 1.4426950408889634
NT = (((1,), (1,)), ((), ()))


def swapped(value):
    return lax.ppermute(value, "guide", [(0, 1), (1, 0)])


def along_z(value, by):
    count = lax.axis_size("seq")
    step = by * ROW
    pairs = [(i, i + step) for i in range(count) if 0 <= i + step < count]
    return lax.ppermute(value, "seq", pairs)


def spread_wide(value):
    count = lax.axis_size("seq")
    groups = [
        [g * count + z * ROW + x for g in range(2) for x in range(ROW)]
        for z in range(count // ROW)
    ]
    return lax.all_to_all(value, ("guide", "seq"), 0, 0, axis_index_groups=groups)


def along_x(value, by):
    count = lax.axis_size("seq")
    pairs = [(i, i // ROW * ROW + (i + by) % ROW) for i in range(count)]
    return lax.ppermute(value, "seq", pairs)


def all_of_row(own):
    middle = own.shape[0] // 2
    return (
        own,
        along_x(own, 1),
        along_x(own, -1),
        along_x(own[:middle], 2),
        along_x(own[middle:], -2),
    )


def spread(value):
    count = lax.axis_size("seq")
    groups = [[z * ROW + x for x in range(ROW)] for z in range(count // ROW)]
    return lax.all_to_all(value, "seq", 0, 0, axis_index_groups=groups)


def gather_weight(copies):
    count = lax.axis_size("seq")
    columns = [[z * ROW + x for z in range(count // ROW)] for x in range(ROW)]
    return lax.all_to_all(copies, "seq", 0, 0, axis_index_groups=columns).reshape(
        -1, copies.shape[2]
    )


def pack_kernel(k_ref, v_ref, kv_out, sems):
    width = kv_out.shape[3]
    copies = []
    for j in range(ROW):
        lanes = pl.ds(j * width, width)
        for i, source in enumerate((k_ref, v_ref)):
            copies.append(
                pltpu.make_async_copy(
                    source.at[0, :, lanes], kv_out.at[j, i], sems.at[len(copies)]
                )
            )
    for copy in copies:
        copy.start()
    for copy in copies:
        copy.wait()


def pack(keys, values):
    _, rows, width = keys.shape
    return pl.pallas_call(
        pack_kernel,
        out_shape=jax.ShapeDtypeStruct((ROW, 2, rows, width // ROW), keys.dtype),
        in_specs=[pl.BlockSpec(memory_space=pl.ANY)] * 2,
        out_specs=pl.BlockSpec(memory_space=pltpu.VMEM),
        scratch_shapes=[pltpu.SemaphoreType.DMA((2 * ROW,))],
        compiler_params=pltpu.CompilerParams(vmem_limit_bytes=56 << 20),
        name="pack",
    )(keys, values)


def request_of(tile, spans, tables):
    start = jnp.int32(0)
    found = [jnp.int32(0) for _ in range(len(tables) + 3)]
    for r in range(spans.shape[0]):
        span = spans[r]
        here = (tile >= start) & (tile < start + span)
        row = [start, span, jnp.int32(r)] + [table(r) for table in tables]
        found = [jnp.where(here, new, old) for new, old in zip(row, found)]
        start = start + span
    return found


def attend_kernel(
    where, spans, text_len, q_ref, far_l, one_l, near_l, own, near_r, one_r, far_r, o_ref, k_all, v_all
):
    place, half = where[0], where[1]
    first = (place // ROW) * ROW
    heads = q_ref.shape[3] // HEAD_WIDTH
    at = 0
    for ref in (far_l, one_l, near_l, own, near_r, one_r, far_r):
        for i in range(ref.shape[0]):
            k_all[at * TILE : (at + 1) * TILE, :] = ref[i, 0]
            v_all[at * TILE : (at + 1) * TILE, :] = ref[i, 1]
            at += 1
    keys = SPAN_MOST * TILE
    column = lax.broadcasted_iota(jnp.int32, (1, keys), 1)
    factor = HEAD_WIDTH**-0.5 * LOG2E
    for t in range(ROW):
        start, span, _, live = request_of(first + t, spans, [lambda r: text_len[half, r]])
        begin = jnp.clip(start - (first - (SPAN_MOST - 1)), 0, SPAN_MOST + ROW - 2)
        begin = pl.multiple_of(begin * TILE, TILE)
        allowed = ((column < live) | (column >= TILE)) & (column < span * TILE)
        bias = jnp.where(allowed, 0.0, -1e30)
        for h in range(heads):
            lanes = slice(h * HEAD_WIDTH, (h + 1) * HEAD_WIDTH)
            key = k_all[pl.ds(begin, keys), lanes]
            value = v_all[pl.ds(begin, keys), lanes]
            score = lax.dot_general(
                q_ref[t, 0, :, lanes], key, NT, preferred_element_type=jnp.float32
            )
            score = score + bias
            top = jnp.max(score, axis=-1, keepdims=True)
            weight = jnp.exp2((score - top) * factor)
            total = jnp.sum(weight, axis=-1, keepdims=True)
            mixed = jnp.dot(weight.astype(jnp.bfloat16), value, preferred_element_type=jnp.float32)
            out = (mixed / total).astype(jnp.bfloat16)
            o_ref[t, :, lanes] = out


def attend(where, spans, text_len, q, parts):
    rows = (SPAN_MOST * 2 + ROW - 2) * TILE
    width = q.shape[3]
    smem = pl.BlockSpec(memory_space=pltpu.SMEM)
    vmem = pl.BlockSpec(memory_space=pltpu.VMEM)
    pairs = ROW * TILE * SPAN_MOST * TILE * (width // HEAD_WIDTH)
    return pl.pallas_call(
        attend_kernel,
        out_shape=jax.ShapeDtypeStruct((ROW, TILE, width), jnp.bfloat16),
        in_specs=[smem] * 3 + [vmem] * 8,
        out_specs=vmem,
        scratch_shapes=[
            pltpu.VMEM((rows, width), jnp.bfloat16),
            pltpu.VMEM((rows, width), jnp.bfloat16),
        ],
        compiler_params=pltpu.CompilerParams(vmem_limit_bytes=58 << 20),
        cost_estimate=pl.CostEstimate(
            flops=4 * pairs * HEAD_WIDTH, bytes_accessed=8 << 20, transcendentals=pairs
        ),
        name="attend",
    )(where, spans, text_len, q, *parts)


def regroup(source, x):
    count = source.shape[0] // SHARD
    starts = [(z * ROW + x) * SHARD for z in range(count // ROW)]
    return jnp.concatenate(
        [source[pl.ds(pl.multiple_of(start, 16), SHARD), :] for start in starts], axis=0
    )


def prepare_kernel(
    where, spans, on, scales, strides, queries, hidden, brought, gate, final_t, latent_t,
    sent, cols, aux, order,
):
    place, half = where[0], where[1]
    x = lax.rem(place, ROW)
    _, _, _, switch, factor, stride = request_of(
        place, spans, [lambda r: on[r], lambda r: scales[r], lambda r: strides[r]]
    )
    channels, width = final_t.shape[0], hidden.shape[2]
    for d in range(ROW):
        sent[d, 0] = queries[0, :, d * width // ROW : (d + 1) * width // ROW]
    for side, rows in enumerate((hidden[half], brought[...])):
        order[...] = rows.astype(jnp.float32).T
        for d in range(ROW):
            sent[d, 1 + side] = regroup(order, d).T.astype(jnp.bfloat16)
    requests = gate.shape[1]
    rest = jnp.zeros((TILE - channels - requests, width), jnp.float32)
    for side, which in enumerate((half, 1 - half)):
        lanes = pl.ds(pl.multiple_of(which * width, 128), width)
        rows = [final_t[:, lanes].astype(jnp.float32)]
        rows += [gate[half, r : r + 1, lanes].astype(jnp.float32) for r in range(requests)]
        order[...] = jnp.concatenate(rows + [rest], axis=0).T
        cols[side] = regroup(order, x).T
    number = lax.broadcasted_iota(jnp.int32, (FULL_WIDTH, TILE), 0).astype(jnp.float32)
    shard = jnp.floor((number + 0.5) * (1.0 / SHARD))
    ring = shard - ROW * jnp.floor((shard + 0.5) * (1.0 / ROW))
    aux[:channels] = latent_t[...]
    for d in range(ROW):
        chosen = jnp.where(ring == d, 1.0, 0.0).astype(jnp.bfloat16)
        aux[(d + 1) * channels : (d + 2) * channels] = jnp.dot(
            final_t[...], chosen, preferred_element_type=jnp.float32
        )
    line = lax.broadcasted_iota(jnp.int32, (8, TILE), 0)
    scalars = jnp.where(line == 1, factor, jnp.where(line == 2, stride, 0.0))
    aux[(ROW + 1) * channels :] = jnp.where(line == 0, switch.astype(jnp.float32), scalars)


def prepare(where, spans, on, scales, strides, queries, hidden, brought, gate, final_t, latent_t):
    width, channels = hidden.shape[2], final_t.shape[0]
    smem = pl.BlockSpec(memory_space=pltpu.SMEM)
    vmem = pl.BlockSpec(memory_space=pltpu.VMEM)
    return pl.pallas_call(
        prepare_kernel,
        out_shape=(
            jax.ShapeDtypeStruct((ROW, 3, TILE, width // ROW), jnp.bfloat16),
            jax.ShapeDtypeStruct((2, TILE, width // ROW), jnp.float32),
            jax.ShapeDtypeStruct(((ROW + 1) * channels + 8, TILE), jnp.float32),
        ),
        in_specs=[smem] * 5 + [vmem] * 6,
        out_specs=(vmem,) * 3,
        scratch_shapes=[pltpu.VMEM((width, TILE), jnp.float32)],
        compiler_params=pltpu.CompilerParams(vmem_limit_bytes=16 << 20),
        name="prepare",
    )(where, spans, on, scales, strides, queries, hidden, brought, gate, final_t, latent_t)


def project_kernel(
    where, spans, own, behind, ahead, far_a, far_b, w_mine, w_other, hidden, cols,
    out, attn, state,
):
    first = where[0] // ROW * ROW
    x = where[0] - first
    tiles, _, depth = own.shape
    middle = far_a.shape[0]
    for ref, step, begin in (
        (own, 0, 0), (behind, ROW - 1, 0), (ahead, 1, 0), (far_a, 2, 0), (far_b, 2, middle)
    ):
        lanes = pl.ds(pl.multiple_of(lax.rem(x + step, ROW) * depth, 128), depth)
        for i in range(ref.shape[0]):
            attn[(begin + i) * TILE : (begin + i + 1) * TILE, lanes] = ref[i]
    channels = out.shape[1] - 8
    block = cols.shape[2]
    for side, weight in enumerate((w_mine, w_other)):
        total = lax.dot_general(attn[...], weight[...], NT, preferred_element_type=jnp.float32)
        for t in range(tiles):
            _, _, request = request_of(first + t, spans, [])
            scale = jnp.zeros((1, block), jnp.float32)
            for r in range(spans.shape[0]):
                row = cols[side, channels + r : channels + r + 1, :]
                scale = jnp.where(request == r, row, scale)
            rows = slice(t * TILE, (t + 1) * TILE)
            state[side, rows] = (
                hidden[t, 1 + side].astype(jnp.float32) + scale * total[rows]
            )
    mean = jnp.sum(state[0], axis=-1, keepdims=True) + jnp.sum(state[1], axis=-1, keepdims=True)
    mean = mean * (1.0 / (2 * block))
    squares = jnp.zeros_like(mean)
    speed = jnp.zeros((tiles * TILE, channels), jnp.float32)
    for side in range(2):
        centre = state[side] - mean
        squares += jnp.sum(centre * centre, axis=-1, keepdims=True)
        high = centre.astype(jnp.bfloat16)
        low = (centre - high.astype(jnp.float32)).astype(jnp.bfloat16)
        final = cols[side, :channels, :].astype(jnp.bfloat16)
        speed += lax.dot_general(high, final, NT, preferred_element_type=jnp.float32)
        speed += lax.dot_general(low, final, NT, preferred_element_type=jnp.float32)
    lane = lax.broadcasted_iota(jnp.int32, (tiles * TILE, TILE - channels), 1)
    extra = jnp.where(lane == 0, mean, jnp.where(lane == 1, squares, 0.0))
    sums = jnp.concatenate([speed, extra], axis=1)
    for t in range(tiles):
        turned = sums[t * TILE : (t + 1) * TILE].T[: channels + 8]
        out[t] = turned
        out[tiles + t] = turned


def project(where, spans, attn, weights, hidden, cols, channels):
    block, depth = weights[0].shape
    tokens = attn[0].shape[0] * TILE
    smem = pl.BlockSpec(memory_space=pltpu.SMEM)
    vmem = pl.BlockSpec(memory_space=pltpu.VMEM)
    return pl.pallas_call(
        project_kernel,
        out_shape=jax.ShapeDtypeStruct((2 * ROW, channels + 8, TILE), jnp.float32),
        in_specs=[smem] * 2 + [vmem] * 9,
        out_specs=vmem,
        scratch_shapes=[
            pltpu.VMEM((tokens, depth), jnp.bfloat16),
            pltpu.VMEM((2, tokens, block), jnp.float32),
        ],
        compiler_params=pltpu.CompilerParams(vmem_limit_bytes=58 << 20),
        cost_estimate=pl.CostEstimate(
            flops=4 * tokens * depth * block, bytes_accessed=8 << 20, transcendentals=0
        ),
        name="project",
    )(where, spans, *attn, *weights, hidden, cols)


def finish_kernel(parts, aux, out_t):
    channels = out_t.shape[0]
    tables = [aux[(d + 1) * channels : (d + 2) * channels, :] for d in range(ROW)]
    last = (ROW + 1) * channels
    switch, factor, stride = (aux[last + i : last + i + 1, :] for i in range(3))
    speeds = []
    for which in range(2):
        four = [parts[which * ROW + d] for d in range(ROW)]
        means = [p[channels : channels + 1] for p in four]
        mean = sum(means) / ROW
        gaps = [m - mean for m in means]
        squares = sum(
            p[channels + 1 : channels + 2] + gap * gap * (FULL_WIDTH / ROW)
            for p, gap in zip(four, gaps)
        )
        raw = sum(p[:channels] + gap * table for p, gap, table in zip(four, gaps, tables))
        speeds.append(raw * lax.rsqrt(squares / FULL_WIDTH + 1e-06))
    cond, uncond = speeds
    blend = jnp.where(switch > 0, uncond + factor * (cond - uncond), cond)
    upper = jnp.sqrt(jnp.mean(cond * cond, axis=0, keepdims=True) + 1e-06)
    lower = jnp.sqrt(jnp.mean(blend * blend, axis=0, keepdims=True) + 1e-06)
    out_t[...] = aux[:channels, :] + stride * (blend * (upper / lower))


def finish(parts, aux, channels):
    vmem = pl.BlockSpec(memory_space=pltpu.VMEM)
    return pl.pallas_call(
        finish_kernel,
        out_shape=jax.ShapeDtypeStruct((channels, TILE), jnp.float32),
        in_specs=[vmem] * 2,
        out_specs=vmem,
        compiler_params=pltpu.CompilerParams(vmem_limit_bytes=4 << 20),
        name="finish",
    )(parts, aux)


def shards(
    queries,
    keys,
    values,
    hidden_in,
    out_weight,
    final_weight,
    gate_mod,
    span_tiles,
    text_len,
    guide_on,
    guide_scale,
    step_size,
    latent,
):
    place = lax.axis_index("seq")
    half = lax.axis_index("guide")
    where = jnp.stack([place, half]).astype(jnp.int32)
    away = lax.dynamic_index_in_dim(hidden_in, 1 - half, 0, keepdims=False)
    brought = swapped(away)
    own = spread(pack(keys, values))
    queries, gate_mod, _ = lax.optimization_barrier((queries, gate_mod, own))
    near_l = along_z(own[1:], 1)
    near_r = along_z(own[:-1], -1)
    one_l = along_z(own[:1], 1)
    one_r = along_z(own[-1:], -1)
    far_l = along_z(near_l, 1)
    far_r = along_z(near_r, -1)
    sent, cols, aux = prepare(
        where,
        span_tiles,
        guide_on,
        guide_scale,
        step_size,
        queries,
        hidden_in,
        brought,
        gate_mod,
        final_weight.T,
        latent.T,
    )
    local = spread(sent)
    parts = (far_l, one_l, near_l, own, near_r, one_r, far_r)
    shard = jnp.broadcast_to(out_weight.T, (lax.axis_size("seq") // ROW, *out_weight.T.shape))
    shard, queries = lax.optimization_barrier((shard, queries))
    shard, *_ = lax.optimization_barrier((shard, *parts))
    weight = gather_weight(shard)
    attn = all_of_row(attend(where, span_tiles, text_len, local, parts))
    weight, attn = lax.optimization_barrier((weight, attn))
    weights = [weight, swapped(weight)]
    channels = latent.shape[1]
    sums = project(where, span_tiles, attn, weights, local, cols, channels)
    return finish(spread_wide(sums), aux, channels).T


def solution(mesh):
    in_specs = (
        P("guide", ("rep", "seq"), None),
        P("guide", ("rep", "seq"), None),
        P("guide", ("rep", "seq"), None),
        P(None, ("rep", "seq"), "guide"),
        P(None, ("guide", "seq")),
        P(),
        P(None, "rep", None),
        P("rep"),
        P(None, "rep"),
        P("rep"),
        P("rep"),
        P("rep"),
        P(("rep", "seq"), None),
    )
    out_specs = P(("rep", "seq"), None)
    return jax.shard_map(shards, mesh=mesh, in_specs=in_specs, out_specs=out_specs, check_vma=False)
```

```python
import jax
import jax.numpy as jnp
from jax import lax
from jax.experimental import pallas as pl
from jax.experimental.pallas import tpu as pltpu
from jax.sharding import PartitionSpec as P

HEAD_WIDTH = 128
TILE = 128
SPAN_MOST = 8
FULL_WIDTH = 3072
SHARD = 48
ROW = 4
LOG2E = 1.4426950408889634
NT = (((1,), (1,)), ((), ()))


def swapped(value):
    return lax.ppermute(value, "guide", [(0, 1), (1, 0)])


def along_z(value, by):
    count = lax.axis_size("seq")
    step = by * ROW
    pairs = [(i, i + step) for i in range(count) if 0 <= i + step < count]
    return lax.ppermute(value, "seq", pairs)


def spread_wide(value):
    count = lax.axis_size("seq")
    groups = [
        [g * count + z * ROW + x for g in range(2) for x in range(ROW)]
        for z in range(count // ROW)
    ]
    return lax.all_to_all(value, ("guide", "seq"), 0, 0, axis_index_groups=groups)


def along_x(value, by):
    count = lax.axis_size("seq")
    pairs = [(i, i // ROW * ROW + (i + by) % ROW) for i in range(count)]
    return lax.ppermute(value, "seq", pairs)


def all_of_row(own):
    middle = own.shape[0] // 2
    return (
        own,
        along_x(own, 1),
        along_x(own, -1),
        along_x(own[:middle], 2),
        along_x(own[middle:], -2),
    )


def spread(value):
    count = lax.axis_size("seq")
    groups = [[z * ROW + x for x in range(ROW)] for z in range(count // ROW)]
    return lax.all_to_all(value, "seq", 0, 0, axis_index_groups=groups)


def gather_weight(copies):
    count = lax.axis_size("seq")
    columns = [[z * ROW + x for z in range(count // ROW)] for x in range(ROW)]
    return lax.all_to_all(copies, "seq", 0, 0, axis_index_groups=columns).reshape(
        -1, copies.shape[2]
    )


def pack_kernel(k_ref, v_ref, kv_out, sems):
    width = kv_out.shape[3]
    copies = []
    for j in range(ROW):
        lanes = pl.ds(j * width, width)
        for i, source in enumerate((k_ref, v_ref)):
            copies.append(
                pltpu.make_async_copy(
                    source.at[0, :, lanes], kv_out.at[j, i], sems.at[len(copies)]
                )
            )
    for copy in copies:
        copy.start()
    for copy in copies:
        copy.wait()


def pack(keys, values):
    _, rows, width = keys.shape
    return pl.pallas_call(
        pack_kernel,
        out_shape=jax.ShapeDtypeStruct((ROW, 2, rows, width // ROW), keys.dtype),
        in_specs=[pl.BlockSpec(memory_space=pl.ANY)] * 2,
        out_specs=pl.BlockSpec(memory_space=pltpu.VMEM),
        scratch_shapes=[pltpu.SemaphoreType.DMA((2 * ROW,))],
        compiler_params=pltpu.CompilerParams(vmem_limit_bytes=56 << 20),
        name="pack",
    )(keys, values)


def request_of(tile, spans, tables):
    start = jnp.int32(0)
    found = [jnp.int32(0) for _ in range(len(tables) + 3)]
    for r in range(spans.shape[0]):
        span = spans[r]
        here = (tile >= start) & (tile < start + span)
        row = [start, span, jnp.int32(r)] + [table(r) for table in tables]
        found = [jnp.where(here, new, old) for new, old in zip(row, found)]
        start = start + span
    return found


def attend_kernel(
    where, spans, text_len, q_ref, far_l, one_l, near_l, own, near_r, one_r, far_r, o_ref,
    k_all, v_all, q_all, arrived,
):
    place, half = where[0], where[1]
    first = (place // ROW) * ROW
    heads = q_ref.shape[3] // HEAD_WIDTH
    copies, at = [], 0
    for ref in (far_l, one_l, near_l, own, near_r, one_r, far_r):
        for i in range(ref.shape[0]):
            for j, whole in enumerate((k_all, v_all)):
                copies.append((ref.at[i, j], whole.at[pl.ds(at * TILE, TILE)]))
            at += 1
    copies += [(q_ref.at[i, 0], q_all.at[i]) for i in range(ROW)]
    copies = [pltpu.make_async_copy(*pair, arrived.at[n]) for n, pair in enumerate(copies)]
    for copy in copies:
        copy.start()
    for copy in copies:
        copy.wait()
    keys = SPAN_MOST * TILE
    column = lax.broadcasted_iota(jnp.int32, (1, keys), 1)
    factor = HEAD_WIDTH**-0.5 * LOG2E
    for t in range(ROW):
        start, span, _, live = request_of(first + t, spans, [lambda r: text_len[half, r]])
        begin = jnp.clip(start - (first - (SPAN_MOST - 1)), 0, SPAN_MOST + ROW - 2)
        begin = pl.multiple_of(begin * TILE, TILE)
        allowed = ((column < live) | (column >= TILE)) & (column < span * TILE)
        bias = jnp.where(allowed, 0.0, -1e30)
        for h in range(heads):
            lanes = slice(h * HEAD_WIDTH, (h + 1) * HEAD_WIDTH)
            key = k_all[pl.ds(begin, keys), lanes]
            value = v_all[pl.ds(begin, keys), lanes]
            score = lax.dot_general(
                q_all[t, :, lanes], key, NT, preferred_element_type=jnp.float32
            )
            score = score + bias
            top = jnp.max(score, axis=-1, keepdims=True)
            weight = jnp.exp2((score - top) * factor)
            total = jnp.sum(weight, axis=-1, keepdims=True)
            mixed = jnp.dot(weight.astype(jnp.bfloat16), value, preferred_element_type=jnp.float32)
            out = (mixed / total).astype(jnp.bfloat16)
            o_ref[t, :, lanes] = out


def attend(where, spans, text_len, q, parts):
    rows = (SPAN_MOST * 2 + ROW - 2) * TILE
    width = q.shape[3]
    smem = pl.BlockSpec(memory_space=pltpu.SMEM)
    vmem = pl.BlockSpec(memory_space=pltpu.VMEM)
    pairs = ROW * TILE * SPAN_MOST * TILE * (width // HEAD_WIDTH)
    return pl.pallas_call(
        attend_kernel,
        out_shape=jax.ShapeDtypeStruct((ROW, TILE, width), jnp.bfloat16),
        in_specs=[smem] * 3 + [pl.BlockSpec(memory_space=pl.ANY)] * 8,
        out_specs=vmem,
        scratch_shapes=[
            pltpu.VMEM((rows, width), jnp.bfloat16),
            pltpu.VMEM((rows, width), jnp.bfloat16),
            pltpu.VMEM((ROW, TILE, width), jnp.bfloat16),
            pltpu.SemaphoreType.DMA((2 * rows // TILE + ROW,)),
        ],
        compiler_params=pltpu.CompilerParams(vmem_limit_bytes=58 << 20),
        cost_estimate=pl.CostEstimate(
            flops=4 * pairs * HEAD_WIDTH, bytes_accessed=8 << 20, transcendentals=pairs
        ),
        name="attend",
    )(where, spans, text_len, q, *parts)


def regroup(source, x):
    count = source.shape[0] // SHARD
    starts = [(z * ROW + x) * SHARD for z in range(count // ROW)]
    return jnp.concatenate(
        [source[pl.ds(pl.multiple_of(start, 16), SHARD), :] for start in starts], axis=0
    )


def prepare_kernel(
    where, spans, on, scales, strides, queries, hidden, brought, gate, final_t, latent_t,
    sent, cols, aux, order,
):
    place, half = where[0], where[1]
    x = lax.rem(place, ROW)
    _, _, _, switch, factor, stride = request_of(
        place, spans, [lambda r: on[r], lambda r: scales[r], lambda r: strides[r]]
    )
    channels, width = final_t.shape[0], hidden.shape[2]
    for d in range(ROW):
        sent[d, 0] = queries[0, :, d * width // ROW : (d + 1) * width // ROW]
    for side, rows in enumerate((hidden[half], brought[...])):
        order[...] = rows.astype(jnp.float32).T
        for d in range(ROW):
            sent[d, 1 + side] = regroup(order, d).T.astype(jnp.bfloat16)
    requests = gate.shape[1]
    rest = jnp.zeros((TILE - channels - requests, width), jnp.float32)
    for side, which in enumerate((half, 1 - half)):
        lanes = pl.ds(pl.multiple_of(which * width, 128), width)
        rows = [final_t[:, lanes].astype(jnp.float32)]
        rows += [gate[half, r : r + 1, lanes].astype(jnp.float32) for r in range(requests)]
        order[...] = jnp.concatenate(rows + [rest], axis=0).T
        cols[side] = regroup(order, x).T
    number = lax.broadcasted_iota(jnp.int32, (FULL_WIDTH, TILE), 0).astype(jnp.float32)
    shard = jnp.floor((number + 0.5) * (1.0 / SHARD))
    ring = shard - ROW * jnp.floor((shard + 0.5) * (1.0 / ROW))
    aux[:channels] = latent_t[...]
    for d in range(ROW):
        chosen = jnp.where(ring == d, 1.0, 0.0).astype(jnp.bfloat16)
        aux[(d + 1) * channels : (d + 2) * channels] = jnp.dot(
            final_t[...], chosen, preferred_element_type=jnp.float32
        )
    line = lax.broadcasted_iota(jnp.int32, (8, TILE), 0)
    scalars = jnp.where(line == 1, factor, jnp.where(line == 2, stride, 0.0))
    aux[(ROW + 1) * channels :] = jnp.where(line == 0, switch.astype(jnp.float32), scalars)


def prepare(where, spans, on, scales, strides, queries, hidden, brought, gate, final_t, latent_t):
    width, channels = hidden.shape[2], final_t.shape[0]
    smem = pl.BlockSpec(memory_space=pltpu.SMEM)
    vmem = pl.BlockSpec(memory_space=pltpu.VMEM)
    return pl.pallas_call(
        prepare_kernel,
        out_shape=(
            jax.ShapeDtypeStruct((ROW, 3, TILE, width // ROW), jnp.bfloat16),
            jax.ShapeDtypeStruct((2, TILE, width // ROW), jnp.float32),
            jax.ShapeDtypeStruct(((ROW + 1) * channels + 8, TILE), jnp.float32),
        ),
        in_specs=[smem] * 5 + [vmem] * 6,
        out_specs=(vmem,) * 3,
        scratch_shapes=[pltpu.VMEM((width, TILE), jnp.float32)],
        compiler_params=pltpu.CompilerParams(vmem_limit_bytes=16 << 20),
        name="prepare",
    )(where, spans, on, scales, strides, queries, hidden, brought, gate, final_t, latent_t)


def project_kernel(
    where, spans, own, behind, ahead, far_a, far_b, w_mine, w_other, hidden, cols,
    out, attn, state,
):
    first = where[0] // ROW * ROW
    x = where[0] - first
    tiles, _, depth = own.shape
    middle = far_a.shape[0]
    for ref, step, begin in (
        (own, 0, 0), (behind, ROW - 1, 0), (ahead, 1, 0), (far_a, 2, 0), (far_b, 2, middle)
    ):
        lanes = pl.ds(pl.multiple_of(lax.rem(x + step, ROW) * depth, 128), depth)
        for i in range(ref.shape[0]):
            attn[(begin + i) * TILE : (begin + i + 1) * TILE, lanes] = ref[i]
    channels = out.shape[1] - 8
    block = cols.shape[2]
    for side, weight in enumerate((w_mine, w_other)):
        total = lax.dot_general(attn[...], weight[...], NT, preferred_element_type=jnp.float32)
        for t in range(tiles):
            _, _, request = request_of(first + t, spans, [])
            scale = jnp.zeros((1, block), jnp.float32)
            for r in range(spans.shape[0]):
                row = cols[side, channels + r : channels + r + 1, :]
                scale = jnp.where(request == r, row, scale)
            rows = slice(t * TILE, (t + 1) * TILE)
            state[side, rows] = (
                hidden[t, 1 + side].astype(jnp.float32) + scale * total[rows]
            )
    mean = jnp.sum(state[0], axis=-1, keepdims=True) + jnp.sum(state[1], axis=-1, keepdims=True)
    mean = mean * (1.0 / (2 * block))
    squares = jnp.zeros_like(mean)
    speed = jnp.zeros((tiles * TILE, channels), jnp.float32)
    for side in range(2):
        centre = state[side] - mean
        squares += jnp.sum(centre * centre, axis=-1, keepdims=True)
        high = centre.astype(jnp.bfloat16)
        low = (centre - high.astype(jnp.float32)).astype(jnp.bfloat16)
        final = cols[side, :channels, :].astype(jnp.bfloat16)
        speed += lax.dot_general(high, final, NT, preferred_element_type=jnp.float32)
        speed += lax.dot_general(low, final, NT, preferred_element_type=jnp.float32)
    lane = lax.broadcasted_iota(jnp.int32, (tiles * TILE, TILE - channels), 1)
    extra = jnp.where(lane == 0, mean, jnp.where(lane == 1, squares, 0.0))
    sums = jnp.concatenate([speed, extra], axis=1)
    for t in range(tiles):
        turned = sums[t * TILE : (t + 1) * TILE].T[: channels + 8]
        out[t] = turned
        out[tiles + t] = turned


def project(where, spans, attn, weights, hidden, cols, channels):
    block, depth = weights[0].shape
    tokens = attn[0].shape[0] * TILE
    smem = pl.BlockSpec(memory_space=pltpu.SMEM)
    vmem = pl.BlockSpec(memory_space=pltpu.VMEM)
    return pl.pallas_call(
        project_kernel,
        out_shape=jax.ShapeDtypeStruct((2 * ROW, channels + 8, TILE), jnp.float32),
        in_specs=[smem] * 2 + [vmem] * 9,
        out_specs=vmem,
        scratch_shapes=[
            pltpu.VMEM((tokens, depth), jnp.bfloat16),
            pltpu.VMEM((2, tokens, block), jnp.float32),
        ],
        compiler_params=pltpu.CompilerParams(vmem_limit_bytes=58 << 20),
        cost_estimate=pl.CostEstimate(
            flops=4 * tokens * depth * block, bytes_accessed=8 << 20, transcendentals=0
        ),
        name="project",
    )(where, spans, *attn, *weights, hidden, cols)


def finish_kernel(parts, aux, out_t):
    channels = out_t.shape[0]
    tables = [aux[(d + 1) * channels : (d + 2) * channels, :] for d in range(ROW)]
    last = (ROW + 1) * channels
    switch, factor, stride = (aux[last + i : last + i + 1, :] for i in range(3))
    speeds = []
    for which in range(2):
        four = [parts[which * ROW + d] for d in range(ROW)]
        means = [p[channels : channels + 1] for p in four]
        mean = sum(means) / ROW
        gaps = [m - mean for m in means]
        squares = sum(
            p[channels + 1 : channels + 2] + gap * gap * (FULL_WIDTH / ROW)
            for p, gap in zip(four, gaps)
        )
        raw = sum(p[:channels] + gap * table for p, gap, table in zip(four, gaps, tables))
        speeds.append(raw * lax.rsqrt(squares / FULL_WIDTH + 1e-06))
    cond, uncond = speeds
    blend = jnp.where(switch > 0, uncond + factor * (cond - uncond), cond)
    upper = jnp.sqrt(jnp.mean(cond * cond, axis=0, keepdims=True) + 1e-06)
    lower = jnp.sqrt(jnp.mean(blend * blend, axis=0, keepdims=True) + 1e-06)
    out_t[...] = aux[:channels, :] + stride * (blend * (upper / lower))


def finish(parts, aux, channels):
    vmem = pl.BlockSpec(memory_space=pltpu.VMEM)
    return pl.pallas_call(
        finish_kernel,
        out_shape=jax.ShapeDtypeStruct((channels, TILE), jnp.float32),
        in_specs=[vmem] * 2,
        out_specs=vmem,
        compiler_params=pltpu.CompilerParams(vmem_limit_bytes=4 << 20),
        name="finish",
    )(parts, aux)


def shards(
    queries,
    keys,
    values,
    hidden_in,
    out_weight,
    final_weight,
    gate_mod,
    span_tiles,
    text_len,
    guide_on,
    guide_scale,
    step_size,
    latent,
):
    place = lax.axis_index("seq")
    half = lax.axis_index("guide")
    where = jnp.stack([place, half]).astype(jnp.int32)
    away = lax.dynamic_index_in_dim(hidden_in, 1 - half, 0, keepdims=False)
    brought = swapped(away)
    own = spread(pack(keys, values))
    queries, gate_mod, _ = lax.optimization_barrier((queries, gate_mod, own))
    near_l = along_z(own[1:], 1)
    near_r = along_z(own[:-1], -1)
    one_l = along_z(own[:1], 1)
    one_r = along_z(own[-1:], -1)
    far_l = along_z(near_l, 1)
    far_r = along_z(near_r, -1)
    sent, cols, aux = prepare(
        where,
        span_tiles,
        guide_on,
        guide_scale,
        step_size,
        queries,
        hidden_in,
        brought,
        gate_mod,
        final_weight.T,
        latent.T,
    )
    local = spread(sent)
    parts = (far_l, one_l, near_l, own, near_r, one_r, far_r)
    shard = jnp.broadcast_to(out_weight.T, (lax.axis_size("seq") // ROW, *out_weight.T.shape))
    shard, queries = lax.optimization_barrier((shard, queries))
    shard, *_ = lax.optimization_barrier((shard, *parts))
    weight = gather_weight(shard)
    attn = all_of_row(attend(where, span_tiles, text_len, local, parts))
    weight, attn = lax.optimization_barrier((weight, attn))
    weights = [weight, swapped(weight)]
    channels = latent.shape[1]
    sums = project(where, span_tiles, attn, weights, local, cols, channels)
    return finish(spread_wide(sums), aux, channels).T


def solution(mesh):
    in_specs = (
        P("guide", ("rep", "seq"), None),
        P("guide", ("rep", "seq"), None),
        P("guide", ("rep", "seq"), None),
        P(None, ("rep", "seq"), "guide"),
        P(None, ("guide", "seq")),
        P(),
        P(None, "rep", None),
        P("rep"),
        P(None, "rep"),
        P("rep"),
        P("rep"),
        P("rep"),
        P(("rep", "seq"), None),
    )
    out_specs = P(("rep", "seq"), None)
    return jax.shard_map(shards, mesh=mesh, in_specs=in_specs, out_specs=out_specs, check_vma=False)
```
